512 devices in a mesh: row: 32 (over z_lo, x), col: 16 (over y, z_hi, core).
Axes of the slice: x: 4, y: 4, z: 16 (z_hi: 2, z_lo: 8; z = z_hi * 8 + z_lo), core: 2. Of those that a mesh axis runs over, the one named last changes fastest.
Arguments:
- temp_in: float32 [2304, 16, 4608], P('row', 'col'), may hold values from -6 to 6
- velocity: bfloat16 [3, 16, 4608, 1536], P(None, 'col', 'row'), may hold values from -3 to 3
- spacing_x: float32 [1536], replicated, may hold values from 0.3 to 3
- inverse_x: float32 [12, 128, 128], replicated
- link_x: float32 [11], replicated, may hold values from 0.3 to 1.5
- inverse_z: float32 [36, 128, 128], replicated
- link_z: float32 [35], replicated, may hold values from 0.3 to 1.5
- counts_in: int32 [32], replicated, may hold values from 1 to 72, 1536 in all
- counts_out: int32 [32], replicated, may hold values from 1 to 72, 1536 in all
Outputs:
- temp_out: float32 [2304, 16, 4608], P('row', 'col')
The draws below stay inside these ranges and needn't reach their ends.
Inputs may be any that keep to these rules, and one draw needn't show every extreme that they name: counts_in sums to 1536; some entry equals 72. counts_out sums to 1536; some entry equals 72.
All inputs are finite; a program needn't handle non-finite values.
Results may differ from the reference program's by a relative error of at most 0.0003.
Values sent between devices are 32-bit elements; how exact they have to be, the bound alone decides.
A program may use at most 64 MiB of HBM per device.

```python
import math
import jax
import jax.numpy as jnp
import numpy as np
from jax import lax

NX = 1536
NZ = 4608
NY = 16
BLOCK = 128
KX = 12
KZ = 36
SLOT_R = 72
SLOT_C = 72
N_ROW = 32


def banded_blocks(key, count, order, lower_end, upper_end):
    places = jnp.arange(order)
    distance = jnp.abs(places[:, None] - places[None, :]).astype(jnp.float32)
    reach = max(order // 8, 2)
    rough = jax.random.uniform(key, (count, order, order), jnp.float32, lower_end, upper_end)
    shape_part = jnp.exp(-distance / reach) / math.sqrt(reach)
    return jnp.eye(order, dtype=jnp.float32)[None] + shape_part[None] * rough


def draw_inverse_x(key, part):
    key = jax.random.fold_in(key, 11)
    return banded_blocks(key, KX, BLOCK, 0.5, 1.5)


def draw_inverse_z(key, part):
    key = jax.random.fold_in(key, 13)
    return banded_blocks(key, KZ, BLOCK, 0.5, 1.5)


def steps_of(key, dims, shards, low, top_value):
    loudness = 1.0
    for axis_at, shards_of in shards:
        steps = jax.random.uniform(jax.random.fold_in(jax.random.fold_in(key, 6), axis_at), (shards_of,), jnp.float32, low / len(shards), top_value / len(shards))
        loudness = loudness * jnp.repeat(jnp.exp(steps), dims[axis_at] // shards_of).reshape((-1,) + (1,) * (len(dims) - 1 - axis_at))
    return loudness


def profile(amount, total, bound, skew):
    portions = [(1 << 20) // math.isqrt(rank ** skew) + 1 for rank in range(2, amount + 1)]
    spare, given = total - bound - (amount - 1), [1] * (amount - 1)
    while spare > 0:
        candidates = [i for i in range(amount - 1) if given[i] < bound]
        pool, left = sum([portions[i] for i in candidates]), spare
        for i in candidates:
            more = min(bound - given[i], max(1, left * portions[i] // pool), spare)
            given[i] = given[i] + more
            spare = spare - more
    return np.array([bound] + given)


def ragged(key, count, total, bound, slope):
    if count == 2:
        one = jax.random.randint(key, (), max(1, total - bound), min(bound, total - 1) + 1)
        return jnp.stack([one, total - one])
    tallies = jnp.asarray(profile(count, total, bound, slope), jnp.int32)
    pairs = (count - 1) // 2
    giver, sink = tallies[1:1 + 2 * pairs:2], tallies[2:2 + 2 * pairs:2]
    margin = jnp.minimum(giver - 1, bound - sink)
    shifted = jax.random.randint(jax.random.fold_in(key, 1), (pairs,), 0, 1 << 20) % (margin + 1)
    tallies = tallies.at[1:1 + 2 * pairs:2].set(giver - shifted).at[2:2 + 2 * pairs:2].set(sink + shifted)
    return tallies[jax.random.permutation(jax.random.fold_in(key, 2), count)]


def normal_values(stream_key, dims, deviation, bound, cuts=(), kind=jnp.bfloat16):
    array = deviation * jax.random.normal(stream_key, dims, jnp.float32)
    if cuts:
        array = array * steps_of(stream_key, dims, cuts, -0.22, 0.18)
    return jnp.clip(array, -bound, bound).astype(kind)


def setup_inputs(seed: int = 0) -> dict:
    arg_keys = jax.random.split(jax.random.key(seed), 10)
    temp_in = normal_values(arg_keys[0], (N_ROW * SLOT_R, NY, NZ), 1.0, 6.0, ((0, 32), (1, 16)), jnp.float32)
    velocity = normal_values(arg_keys[1], (3, NY, NZ, NX), 0.5, 3.0, ((1, 16), (2, 32)))
    spacing_x = jnp.clip(jnp.exp(jax.random.uniform(arg_keys[2], (NX,), jnp.float32, math.log(0.3), math.log(3.0))), 0.3, 3.0)
    inverse_x = draw_inverse_x(jax.random.fold_in(arg_keys[9], 71), 0)
    link_x = jnp.clip(jnp.exp(jax.random.uniform(arg_keys[4], (KX - 1,), jnp.float32, math.log(0.3), math.log(1.5))), 0.3, 1.5)
    inverse_z = draw_inverse_z(jax.random.fold_in(arg_keys[9], 71), 0)
    link_z = jnp.clip(jnp.exp(jax.random.uniform(arg_keys[6], (KZ - 1,), jnp.float32, math.log(0.3), math.log(1.5))), 0.3, 1.5)
    counts_in = ragged(arg_keys[7], N_ROW, NX, SLOT_R, 2).astype(jnp.int32)
    counts_out = ragged(arg_keys[8], N_ROW, NX, SLOT_C, 2).astype(jnp.int32)
    return dict(temp_in=temp_in, velocity=velocity, spacing_x=spacing_x, inverse_x=inverse_x, link_x=link_x, inverse_z=inverse_z, link_z=link_z, counts_in=counts_in, counts_out=counts_out)


def slot_positions(counts, slot_count, planes):
    slot_ends = jnp.cumsum(counts).astype(jnp.int32)
    slot_starts = (slot_ends - counts).astype(jnp.int32)
    owner_row = jnp.sum((planes[:, None] >= slot_ends[None, :]).astype(jnp.int32), axis=1).astype(jnp.int32)
    member = jnp.arange(counts.shape[0], dtype=jnp.int32)[None, :] == owner_row[:, None]
    start_of = jnp.sum(jnp.where(member, slot_starts[None, :], 0), axis=1).astype(jnp.int32)
    return (owner_row * slot_count + planes - start_of).astype(jnp.int32)


def exit_planes(counts, slot_count, plane_count):
    slots = jnp.arange(counts.shape[0] * slot_count, dtype=jnp.int32)
    owner_col = (slots // slot_count).astype(jnp.int32)
    within = (slots % slot_count).astype(jnp.int32)
    slot_starts = (jnp.cumsum(counts) - counts).astype(jnp.int32)
    member = jnp.arange(counts.shape[0], dtype=jnp.int32)[None, :] == owner_col[:, None]
    start_of = jnp.sum(jnp.where(member, slot_starts[None, :], 0), axis=1).astype(jnp.int32)
    count_of = jnp.sum(jnp.where(member, counts[None, :], 0), axis=1).astype(jnp.int32)
    valid = within < count_of
    target = jnp.minimum(start_of + within, plane_count - 1).astype(jnp.int32)
    return target, valid


def linear_scan(coef, values, reverse):
    def combine(earlier, later):
        return (earlier[0] * later[0], later[0] * earlier[1] + later[1])

    return lax.associative_scan(combine, (coef, values), reverse=reverse, axis=values.ndim - 1)[1]


def chain_solve(rhs, inverse, link):
    high = lax.Precision.HIGHEST
    solved = jnp.einsum("...kb,kmb->...km", rhs, inverse, precision=high)
    zero = jnp.zeros_like(link[:1])
    lower = jnp.concatenate([zero, link])
    upper = jnp.concatenate([link, zero])
    fwd_coef = jnp.broadcast_to(lower * inverse[:, -1, 0], solved.shape[:-1])
    ends = linear_scan(fwd_coef, solved[..., -1], False)
    before = jnp.concatenate([jnp.zeros_like(ends[..., :1]), ends[..., :-1]], axis=-1)
    forward = solved + (lower[:, None] * inverse[:, :, 0]) * before[..., None]
    back_coef = jnp.broadcast_to(upper * inverse[:, 0, -1], solved.shape[:-1])
    heads = linear_scan(back_coef, forward[..., 0], True)
    after = jnp.concatenate([heads[..., 1:], jnp.zeros_like(heads[..., :1])], axis=-1)
    return forward + (upper[:, None] * inverse[:, :, -1]) * after[..., None]


def reference(temp_in, velocity, spacing_x, inverse_x, link_x, inverse_z, link_z, counts_in, counts_out):
    planes = jnp.arange(NX, dtype=jnp.int32)
    slot_index = slot_positions(counts_in, SLOT_R, planes)
    field = jnp.take(temp_in, slot_index, axis=0)
    flow_f = jnp.transpose(velocity.astype(jnp.float32), (0, 3, 1, 2))
    padded = jnp.pad(field, ((1, 1), (0, 0), (0, 0)))
    grad_x = (padded[2:] - padded[:-2]) * spacing_x[:, None, None]
    grad_y = jnp.roll(field, -1, 1) - jnp.roll(field, 1, 1)
    grad_z = jnp.roll(field, -1, 2) - jnp.roll(field, 1, 2)
    advection = flow_f[0] * grad_x + 0.5 * (flow_f[1] * grad_y) + 0.5 * (flow_f[2] * grad_z)
    right_side = field - advection
    lines_x = jnp.transpose(right_side, (1, 2, 0)).reshape(NY, NZ, KX, BLOCK)
    after_x = chain_solve(lines_x, inverse_x, link_x).reshape(NY, NZ, NX)
    lines_z = jnp.transpose(after_x, (2, 0, 1)).reshape(NX, NY, KZ, BLOCK)
    after_z = chain_solve(lines_z, inverse_z, link_z).reshape(NX, NY, NZ)
    target, valid = exit_planes(counts_out, SLOT_C, NX)
    picked = jnp.take(after_z, target, axis=0)
    return jnp.where(valid[:, None, None], picked, jnp.zeros_like(picked))
```

```python
import functools
import jax
import jax.numpy as jnp
from jax import lax
from jax.experimental import pallas as pl
from jax.experimental.pallas import tpu as pltpu
from jax.sharding import PartitionSpec as P

MESH = pl.DeviceIdType.MESH
HIGH = lax.Precision.HIGH
B = 128
NQ = 8
QX = 4
ZL = 144
SLOTS = 72
KX = 12
KZ = 36
NT = 3
HALO = 8
FIELD_TILES = KX + NT
F32 = jnp.float32
LIMIT = 48 * 2**20


def here():
    row = lax.axis_index("row")
    return row // QX, row % QX, lax.axis_index("col")


def prefix(counts, first, number):
    total = jnp.int32(0)
    for i in range(number):
        total = total + counts[first + i]
    return total


def quad_starts(counts):
    starts, total = [], jnp.int32(0)
    for q in range(NQ):
        starts.append(total)
        total = total + prefix(counts, QX * q, QX)
    return starts


def offsets(counts, q):
    out, total = [], jnp.int32(0)
    for i in range(QX):
        out.append(total)
        total = total + counts[QX * q + i]
    return out


def own_offset(counts, q, x):
    total = jnp.int32(0)
    for i in range(QX - 1):
        total = total + jnp.where(i < x, counts[QX * q + i], 0)
    return total


def turn_kernel(counts, temp, out):
    q, x, _ = here()
    shift = own_offset(counts, q, x) % B
    pad = jnp.zeros((B - SLOTS, B), F32)
    for k in range(KZ):
        block = temp[pl.ds(k, SLOTS, stride=KZ), :]
        turned = jnp.concatenate([block, pad], axis=0).T
        out[HALO + B * k : HALO + B * (k + 1), :] = pltpu.roll(turned, shift, 1)
    total = KZ * B
    out[0:HALO, :] = out[total : total + HALO, :]
    out[total + HALO : total + 2 * HALO, :] = out[HALO : 2 * HALO, :]


def across(c):
    return jnp.where(c % 2 == 1, (c + 1) % 16, (c + 15) % 16)


def barrier(partners):
    sem = pltpu.get_barrier_semaphore()
    for row, col in partners:
        pl.semaphore_signal(
            sem, inc=1, device_id={"row": row, "col": col}, device_id_type=MESH
        )
    pl.semaphore_wait(sem, len(partners))


def remote(src, dst, send, recv, row, col):
    return pltpu.make_async_remote_copy(
        src_ref=src,
        dst_ref=dst,
        send_sem=send,
        recv_sem=recv,
        device_id={"row": row, "col": col},
        device_id_type=MESH,
    )


ORDER = (7, 6, 5, 4, 3, 2, 1, 0)


def entry_kernel(
    tiles, counts, turned, own, cross, mate, xin, merged,
    x_send, x_recv, x_local, o_send, o_recv, c_send, c_recv, m_send, m_recv, o_local,
):
    q, x, c = here()
    other, twin = across(c), c + 1 - 2 * (c % 2)
    row = QX * q + x
    wide = tiles * B
    partners = [(QX * q + (x + s) % QX, c) for s in range(1, QX)]
    partners += [(QX * ((q + s) % NQ) + x, c) for s in range(1, NQ)]
    partners += [(QX * ((q + s) % NQ) + x, other) for s in range(NQ)]
    partners += [(row, twin)]
    barrier(partners)
    span = ZL + 2 * HALO

    def piece(to_q, to_x):
        start = pl.multiple_of(QX * ZL * to_q + ZL * to_x, 8)
        return turned.at[pl.ds(start, span), :]

    started = []
    x_copies = {}
    for s in ORDER:
        to_q = (q + s) % NQ
        local = pltpu.make_async_copy(piece(to_q, x), xin.at[x, s], x_local.at[s])
        local.start()
        copies = [local]
        for d in range(1, QX):
            to_x = (x + d) % QX
            cp = remote(
                piece(to_q, to_x), xin.at[x, s], x_send.at[d, s], x_recv.at[d, s],
                QX * q + to_x, c,
            )
            cp.start()
            copies.append(cp)
        x_copies[s] = copies
    offs = offsets(counts, q)
    cnts = [counts[QX * q + i] for i in range(QX)]
    lane = lax.broadcasted_iota(jnp.int32, (8, B), 1)
    sub = lax.broadcasted_iota(jnp.int32, (8, B), 0)
    takes = []
    for t in range(tiles):
        at = lane + B * t
        takes.append([(at >= offs[i]) & (at < offs[i] + cnts[i]) for i in range(QX)])
    o_copies, c_copies = {}, {}
    for s in ORDER:
        to_q = (q + s) % NQ
        x_copies[s][0].wait()
        for cp in x_copies[s][1:]:
            cp.wait_recv()

        def put(to_row, parts):
            for t in range(tiles):
                value = jnp.zeros((8, B), F32)
                for i in range(QX):
                    value = jnp.where(takes[t][i], parts[i], value)
                merged[s, pl.ds(to_row, 8), B * t : B * (t + 1)] = value

        def step(j, carry):
            r0 = pl.multiple_of(8 * j, 8)
            put(r0, [xin[i, s, pl.ds(r0 + HALO, 8), :] for i in range(QX)])
            return carry

        lax.fori_loop(0, ZL // 8, step, 0)
        put(
            ZL,
            [
                jnp.where(
                    sub == 7, xin[i, s, 0:HALO, :], xin[i, s, ZL + HALO : ZL + 2 * HALO, :]
                )
                for i in range(QX)
            ],
        )
        if s:
            cp = remote(
                merged.at[s, :, 0:wide], own.at[q, :, 0:wide], o_send.at[s], o_recv.at[s],
                QX * to_q + x, c,
            )
        else:
            cp = pltpu.make_async_copy(
                merged.at[s, :, 0:wide], own.at[q, :, 0:wide], o_local.at[0]
            )
        cp.start()
        o_copies[s] = cp
        cp = remote(
            merged.at[s, 0:ZL, 0:wide], cross.at[q, :, 0:wide], c_send.at[s], c_recv.at[s],
            QX * to_q + x, other,
        )
        cp.start()
        c_copies[s] = cp
    m_copies = {}
    for s in range(NQ):
        from_q = (q + NQ - s) % NQ
        if s:
            o_copies[s].wait_recv()
        else:
            o_copies[s].wait()
        cp = remote(
            own.at[from_q, 0:ZL, 0:wide], mate.at[from_q, :, 0:wide],
            m_send.at[s], m_recv.at[s], row, twin,
        )
        cp.start()
        m_copies[s] = cp
    for s in range(NQ):
        m_copies[s].wait()
        c_copies[s].wait()
        if s:
            o_copies[s].wait_send()
        for cp in x_copies[s][1:]:
            cp.wait_send()


def entry(tiles, cid, counts, turned):
    dma = pltpu.SemaphoreType.DMA
    span = ZL + 2 * HALO
    return pl.pallas_call(
        functools.partial(entry_kernel, tiles),
        name="entry%d" % tiles,
        out_shape=(
            jax.ShapeDtypeStruct((NQ, ZL + HALO, NT * B), F32),
            jax.ShapeDtypeStruct((NQ, ZL, NT * B), F32),
            jax.ShapeDtypeStruct((NQ, ZL, NT * B), F32),
        ),
        in_specs=[
            pl.BlockSpec(memory_space=pltpu.SMEM),
            pl.BlockSpec(memory_space=pltpu.VMEM),
        ],
        out_specs=[pl.BlockSpec(memory_space=pl.ANY)] * 3,
        scratch_shapes=[
            pltpu.VMEM((QX, NQ, span, B), F32),
            pltpu.VMEM((NQ, ZL + HALO, NT * B), F32),
            dma((QX, NQ)), dma((QX, NQ)), dma((NQ,)),
            dma((NQ,)), dma((NQ,)), dma((NQ,)), dma((NQ,)), dma((NQ,)), dma((NQ,)),
            dma((1,)),
        ],
        compiler_params=pltpu.CompilerParams(
            collective_id=cid, has_side_effects=True, vmem_limit_bytes=LIMIT
        ),
    )(counts, turned)


def middle_kernel(
    counts_in, counts_out, link, own, cross, mate, vel, spacing, inverse, out,
    field, diff, right, solved, coef,
):
    c = lax.axis_index("col")
    starts = quad_starts(counts_in)
    lane = lax.broadcasted_iota(jnp.int32, (1, B), 1)

    def place(dst, first, start, parts):
        shift = start % B
        base = pl.multiple_of(start - shift, B)
        keep = lane >= shift
        rolled = [pltpu.roll(part, shift, 1) for part in parts]
        rows = pl.ds(first, parts[0].shape[0])
        dst[rows, pl.ds(base, B)] = jnp.where(keep, rolled[0], dst[rows, pl.ds(base, B)])
        for t in range(1, NT):
            dst[rows, pl.ds(base + B * t, B)] = jnp.where(keep, rolled[t], rolled[t - 1])
        dst[rows, pl.ds(base + B * NT, B)] = rolled[NT - 1]

    sign = jnp.where(c % 2 == 0, F32(1), F32(-1))
    for q in range(NQ):
        place(field, HALO, starts[q], [own[q, :, B * t : B * (t + 1)] for t in range(NT)])
        place(
            diff,
            0,
            starts[q],
            [
                (mate[q, :, B * t : B * (t + 1)] - cross[q, :, B * t : B * (t + 1)]) * sign
                for t in range(NT)
            ],
        )
    field[HALO - 1 : HALO, :] = field[ZL + 2 * HALO - 1 : ZL + 2 * HALO, :]
    nx = KX * B
    step = 16
    at = lax.broadcasted_iota(jnp.int32, (step, nx), 1)
    scale = spacing[...]
    for i in range(ZL // step):
        r0 = HALO + step * i
        here_f = field[r0 : r0 + step, 0:nx]
        low = jnp.where(at == 0, 0.0, pltpu.roll(here_f, 1, 1))
        high = jnp.where(at == nx - 1, 0.0, pltpu.roll(here_f, nx - 1, 1))
        grad_z = field[r0 + 1 : r0 + 1 + step, 0:nx] - field[r0 - 1 : r0 - 1 + step, 0:nx]
        grad_y = diff[step * i : step * (i + 1), 0:nx]
        u, v, w = [vel[j, step * i : step * (i + 1), :].astype(F32) for j in range(3)]
        advection = u * ((high - low) * scale) + 0.5 * (v * grad_y) + 0.5 * (w * grad_z)
        right[step * i : step * (i + 1), :] = here_f - advection
    end = None
    for k in range(KX):
        turned = inverse[k].T
        y = jnp.dot(
            right[:, B * k : B * (k + 1)], turned, precision=HIGH, preferred_element_type=F32
        )
        if k:
            y = y + (link[k - 1] * turned[0:1, :]) * end
        if k < KX - 1:
            coef[k : k + 1, :] = link[k] * turned[B - 1 : B, :]
        end = y[:, B - 1 : B]
        solved[:, B * k : B * (k + 1)] = y
    head = None
    for k in reversed(range(KX)):
        y = solved[:, B * k : B * (k + 1)]
        if k < KX - 1:
            y = y + coef[k : k + 1, :] * head
            solved[:, B * k : B * (k + 1)] = y
        head = y[:, 0:1]
    goals = quad_starts(counts_out)
    for q in range(NQ):
        shift = goals[q] % B
        base = pl.multiple_of(goals[q] - shift, B)
        back = (B - shift) % B
        keep = lane < B - shift
        rolled = [
            pltpu.roll(solved[:, pl.ds(base + B * t, B)], back, 1) for t in range(NT + 1)
        ]
        for t in range(NT):
            out[q, :, B * t : B * (t + 1)] = jnp.where(keep, rolled[t], rolled[t + 1])


def middle(counts_in, counts_out, link, own, cross, mate, vel, spacing, inverse):
    vmem = pl.BlockSpec(memory_space=pltpu.VMEM)
    smem = pl.BlockSpec(memory_space=pltpu.SMEM)
    wide = FIELD_TILES * B
    return pl.pallas_call(
        middle_kernel,
        name="middle",
        out_shape=jax.ShapeDtypeStruct((NQ, ZL, NT * B), F32),
        in_specs=[smem] * 3 + [vmem] * 6,
        out_specs=vmem,
        scratch_shapes=[
            pltpu.VMEM((ZL + 2 * HALO, wide), F32),
            pltpu.VMEM((ZL, wide), F32),
            pltpu.VMEM((ZL, KX * B), F32),
            pltpu.VMEM((ZL, wide), F32),
            pltpu.VMEM((KX + 4, B), F32),
        ],
        compiler_params=pltpu.CompilerParams(vmem_limit_bytes=LIMIT),
    )(counts_in, counts_out, link, own, cross, mate, vel, spacing, inverse)


def exit_kernel(
    tiles, counts, packed, out, rz, piece,
    z_send, z_recv, x_send, x_recv, x_local,
):
    q, x, c = here()
    wide = tiles * B
    partners = [(QX * q + (x + s) % QX, c) for s in range(1, QX)]
    partners += [(QX * ((q + s) % NQ) + x, c) for s in range(1, NQ)]
    barrier(partners)
    z_copies = {}
    for s in range(NQ - 1, 0, -1):
        to_q = (q + s) % NQ
        cp = remote(
            packed.at[to_q, :, 0:wide], rz.at[q, :, 0:wide], z_send.at[s], z_recv.at[s],
            QX * to_q + x, c,
        )
        cp.start()
        z_copies[s] = cp
    offs = offsets(counts, q)
    lane = lax.broadcasted_iota(jnp.int32, (8, B), 1)
    x_copies = []
    for s in range(NQ):
        from_q = (q + NQ - s) % NQ
        if s:
            z_copies[s].wait_recv()
        for d in range(QX):
            to_x = (x + d) % QX
            off = own_offset(counts, q, to_x)
            takes = [(lane + B * t >= off) & (lane + B * t < off + B) for t in range(tiles)]

            def step(j, carry):
                rows = pl.ds(pl.multiple_of(8 * j, 8), 8)
                value = jnp.zeros((8, B), F32)
                for t in range(tiles):
                    cols = slice(B * t, B * (t + 1))
                    if s:
                        part = rz[from_q, rows, cols]
                    else:
                        part = packed[q, rows, cols]
                    value = jnp.where(takes[t], part, value)
                piece[d, s, rows, :] = value
                return carry

            lax.fori_loop(0, ZL // 8, step, 0)
            first = pl.multiple_of(ZL * (QX * from_q + x), 8)
            if d:
                cp = remote(
                    piece.at[d, s], out.at[pl.ds(first, ZL), :],
                    x_send.at[d, s], x_recv.at[d, s], QX * q + to_x, c,
                )
            else:
                cp = pltpu.make_async_copy(
                    piece.at[d, s], out.at[pl.ds(first, ZL), :], x_local.at[s]
                )
            cp.start()
            x_copies.append(cp)
    for cp in x_copies:
        cp.wait()
    for s in range(1, NQ):
        z_copies[s].wait_send()


def leave(tiles, cid, counts, packed):
    dma = pltpu.SemaphoreType.DMA
    return pl.pallas_call(
        functools.partial(exit_kernel, tiles),
        name="leave%d" % tiles,
        out_shape=jax.ShapeDtypeStruct((KZ * B, B), F32),
        in_specs=[
            pl.BlockSpec(memory_space=pltpu.SMEM),
            pl.BlockSpec(memory_space=pltpu.VMEM),
        ],
        out_specs=pl.BlockSpec(memory_space=pl.ANY),
        scratch_shapes=[
            pltpu.VMEM((NQ, ZL, NT * B), F32),
            pltpu.VMEM((QX, NQ, ZL, B), F32),
            dma((NQ,)), dma((NQ,)), dma((QX, NQ)), dma((QX, NQ)), dma((NQ,)),
        ],
        compiler_params=pltpu.CompilerParams(
            collective_id=cid, has_side_effects=True, vmem_limit_bytes=LIMIT
        ),
    )(counts, packed)


def last_kernel(counts, link, lines, inverse, out, solved):
    q, x, _ = here()
    off = own_offset(counts, q, x)
    back = (B - off % B) % B
    count = counts[QX * q + x]
    valid = lax.broadcasted_iota(jnp.int32, (SLOTS, B), 0) < count
    end = None
    for k in range(KZ):
        y = jnp.dot(
            inverse[k], lines[B * k : B * (k + 1), :], precision=HIGH,
            preferred_element_type=F32,
        )
        if k:
            y = y + (link[k - 1] * inverse[k, :, 0:1]) * end
        end = y[B - 1 : B, :]
        solved[B * k : B * (k + 1), :] = y
    head = None
    for k in reversed(range(KZ)):
        y = solved[B * k : B * (k + 1), :]
        if k < KZ - 1:
            y = y + (link[k] * inverse[k, :, B - 1 : B]) * head
        head = y[0:1, :]
        turned = pltpu.roll(y, back, 1).T
        out[pl.ds(k, SLOTS, stride=KZ), :] = jnp.where(valid, turned[0:SLOTS, :], 0.0)


def on_device(
    temp_in, velocity, spacing_x, inverse_x, link_x, inverse_z, link_z, counts_in, counts_out
):
    vmem = pl.BlockSpec(memory_space=pltpu.VMEM)
    smem = pl.BlockSpec(memory_space=pltpu.SMEM)
    local = pltpu.CompilerParams(vmem_limit_bytes=LIMIT)
    turned = pl.pallas_call(
        turn_kernel,
        name="turn",
        out_shape=jax.ShapeDtypeStruct((KZ * B + 2 * HALO, B), F32),
        in_specs=[smem, vmem],
        out_specs=vmem,
        compiler_params=local,
    )(counts_in, temp_in.reshape(SLOTS * KZ, B))
    fits_in = jnp.max(jnp.sum(counts_in.reshape(NQ, QX), axis=1)) <= 2 * B
    fits_out = jnp.max(jnp.sum(counts_out.reshape(NQ, QX), axis=1)) <= 2 * B
    own, cross, mate = lax.cond(
        fits_in,
        functools.partial(entry, 2, 1),
        functools.partial(entry, 3, 2),
        counts_in,
        turned,
    )
    packed = middle(
        counts_in, counts_out, link_x, own, cross, mate,
        velocity.reshape(3, ZL, KX * B), spacing_x.reshape(1, KX * B), inverse_x,
    )
    lines = lax.cond(
        fits_out,
        functools.partial(leave, 2, 3),
        functools.partial(leave, 3, 4),
        counts_out,
        packed,
    )
    out = pl.pallas_call(
        last_kernel,
        name="last",
        out_shape=jax.ShapeDtypeStruct((SLOTS * KZ, B), F32),
        in_specs=[smem, smem, vmem, vmem],
        out_specs=vmem,
        scratch_shapes=[pltpu.VMEM((KZ * B, B), F32)],
        compiler_params=local,
    )(counts_out, link_z, lines, inverse_z)
    return out.reshape(SLOTS, 1, KZ * B)


def solution(mesh):
    in_specs = (
        P("row", "col", None),
        P(None, "col", "row", None),
        P(),
        P(),
        P(),
        P(),
        P(),
        P(),
        P(),
    )
    out_specs = P("row", "col", None)
    return jax.shard_map(
        on_device, mesh=mesh, in_specs=in_specs, out_specs=out_specs, check_vma=False
    )
```

```python
import functools
import jax
import jax.numpy as jnp
from jax import lax
from jax.experimental import pallas as pl
from jax.experimental.pallas import tpu as pltpu
from jax.sharding import PartitionSpec as P

MESH = pl.DeviceIdType.MESH
HIGH = lax.Precision.HIGH
B = 128
NQ = 8
QX = 4
ZL = 144
SLOTS = 72
KX = 12
KZ = 36
HALO = 8
NX = KX * B
CHUNKS = ((0, 48), (48, 48), (96, 48))
NC = len(CHUNKS)
F32 = jnp.float32
LIMIT = 48 * 2**20


def here():
    row = lax.axis_index("row")
    return row // QX, row % QX, lax.axis_index("col")


def starts_of(counts):
    starts, total = [], jnp.int32(0)
    for i in range(NQ * QX):
        starts.append(total)
        total = total + counts[i]
    return starts + [total]


def start_at(counts, row):
    total = jnp.int32(0)
    for i in range(NQ * QX - 1):
        total = total + jnp.where(i < row, counts[i], 0)
    return total


def turn_kernel(counts, temp, out):
    q, x, _ = here()
    shift = start_at(counts, QX * q + x) % B
    pad = jnp.zeros((B - SLOTS, B), F32)
    for k in range(KZ):
        block = temp[pl.ds(k, SLOTS, stride=KZ), :]
        turned = jnp.concatenate([block, pad], axis=0).T
        out[HALO + B * k : HALO + B * (k + 1), :] = pltpu.roll(turned, shift, 1)
    total = KZ * B
    out[0:HALO, :] = out[total : total + HALO, :]
    out[total + HALO : total + 2 * HALO, :] = out[HALO : 2 * HALO, :]


def across(c):
    return jnp.where(c % 2 == 1, (c + 1) % 16, (c + 15) % 16)


def barrier(partners):
    sem = pltpu.get_barrier_semaphore()
    for row, col in partners:
        pl.semaphore_signal(
            sem, inc=1, device_id={"row": row, "col": col}, device_id_type=MESH
        )
    pl.semaphore_wait(sem, len(partners))


def remote(src, dst, send, recv, row, col):
    return pltpu.make_async_remote_copy(
        src_ref=src,
        dst_ref=dst,
        send_sem=send,
        recv_sem=recv,
        device_id={"row": row, "col": col},
        device_id_type=MESH,
    )


ORDER = (7, 6, 5, 4, 3, 2, 1, 0)


def quad_tiles(q, most):
    low = max(QX * q, NX - most * (NQ - q))
    high = min(most * (q + 1), NX - QX * (NQ - 1 - q))
    return range(low // B, (high - 1) // B + 1)


def slot_masks(tiles, start, count, lane):
    first, shift = start // B, start % B
    masks = []
    for t in range(tiles):
        at_first = first % tiles == t
        at_second = (first + 1) % tiles == t
        low = jnp.where(at_first, shift, 2 * B)
        high = jnp.where(at_first, shift + count, 0)
        wrap = jnp.where(at_second, shift + count - B, 0)
        masks.append(((lane >= low) & (lane < high)) | (lane < wrap))
    return masks


def flow_kernel(
    tin, tout, counts_in, counts_out, link, turned, vel_hbm, spacing, inv_hbm, out,
    xin, merged, own, cross, mate, vel, inverse, field, edge, diff, right, solved, coef,
    packed, rz, piece,
    load, x_send, x_recv, x_local, o_send, o_recv, o_local, c_send, c_recv, m_send, m_recv,
    z_send, z_recv, y_send, y_recv, y_local,
):
    q, x, c = here()
    other, twin = across(c), c + 1 - 2 * (c % 2)
    row = QX * q + x
    loads = [
        pltpu.make_async_copy(vel_hbm, vel, load.at[0]),
        pltpu.make_async_copy(inv_hbm, inverse, load.at[1]),
    ]
    for cp in loads:
        cp.start()
    partners = [(QX * q + (x + s) % QX, c) for s in range(1, QX)]
    partners += [(QX * ((q + s) % NQ) + x, c) for s in range(1, NQ)]
    partners += [(QX * ((q + s) % NQ) + x, other) for s in range(NQ)]
    partners += [(row, twin)]
    barrier(partners)
    span = ZL + 2 * HALO

    def source(to_q, to_x):
        start = pl.multiple_of(QX * ZL * to_q + ZL * to_x, 8)
        return turned.at[pl.ds(start, span), :]

    x_copies = {}
    for s in ORDER:
        to_q = (q + s) % NQ
        local = pltpu.make_async_copy(source(to_q, x), xin.at[x, s], x_local.at[s])
        local.start()
        x_copies[s] = [local]
        for d in range(1, QX):
            to_x = (x + d) % QX
            cp = remote(
                source(to_q, to_x), xin.at[x, s], x_send.at[d, s], x_recv.at[d, s],
                QX * q + to_x, c,
            )
            cp.start()
            x_copies[s].append(cp)

    lane = lax.broadcasted_iota(jnp.int32, (8, B), 1)
    sub = lax.broadcasted_iota(jnp.int32, (8, B), 0)
    begin, takes = start_at(counts_in, QX * q), []
    for i in range(QX):
        count = counts_in[QX * q + i]
        takes.append(slot_masks(tin, begin, count, lane))
        begin = begin + count

    def send_rows(s, chunk):
        first, size = CHUNKS[chunk]
        to_q = (q + s) % NQ
        o_first = 0 if chunk == 0 else first + HALO
        o_size = size + HALO if chunk == 0 else size
        o_src, o_dst = merged.at[s, o_first : o_first + o_size], own.at[q, o_first : o_first + o_size]
        if s:
            o_copy = remote(
                o_src, o_dst, o_send.at[chunk, s], o_recv.at[chunk, s], QX * to_q + x, c
            )
        else:
            o_copy = pltpu.make_async_copy(o_src, o_dst, o_local.at[chunk])
        o_copy.start()
        c_copy = remote(
            merged.at[s, first + HALO : first + HALO + size], cross.at[q, first : first + size],
            c_send.at[chunk, s], c_recv.at[chunk, s], QX * to_q + x, other,
        )
        c_copy.start()
        return o_copy, c_copy

    o_copies, c_copies = {}, {}
    for s in ORDER:
        x_copies[s][0].wait()
        for cp in x_copies[s][1:]:
            cp.wait_recv()

        def put(to_row, parts):
            for t in range(tin):
                value = jnp.zeros((8, B), F32)
                for i in range(QX):
                    value = jnp.where(takes[i][t], parts[i], value)
                merged[s, pl.ds(to_row, 8), B * t : B * (t + 1)] = value

        def step(j, carry):
            r0 = pl.multiple_of(8 * j, 8) + HALO
            put(r0, [xin[i, s, pl.ds(r0, 8), :] for i in range(QX)])
            return carry

        lax.fori_loop(0, ZL // 8, step, 0)
        edges = []
        for i in range(QX):
            value = jnp.broadcast_to(xin[i, s, HALO - 1 : HALO, :], (8, B))
            rows = [ZL] + [first + size for first, size in CHUNKS[:-1]]
            for n, z in enumerate(rows):
                value = jnp.where(sub == 1 + n, xin[i, s, HALO + z : HALO + z + 1, :], value)
            edges.append(value)
        put(0, edges)
        o_copies[0, s], c_copies[0, s] = send_rows(s, 0)
    for chunk in range(1, NC):
        for s in ORDER:
            o_copies[chunk, s], c_copies[chunk, s] = send_rows(s, chunk)

    line = lax.broadcasted_iota(jnp.int32, (1, B), 1)
    begins_in = starts_of(counts_in)[::QX]
    begins_out = starts_of(counts_out)[::QX]
    sign = jnp.where(c % 2 == 0, F32(1), F32(-1))

    def covers(begins, p, t):
        return (line >= begins[p] - B * t) & (line < begins[p + 1] - B * t)

    def assemble(dst, to, size, read):
        for t in range(KX):
            value = jnp.zeros((size, B), F32)
            for p in range(NQ):
                if t in quad_tiles(p, most_in):
                    value = jnp.where(covers(begins_in, p, t), read(p, t % tin), value)
            dst[to : to + size, B * t : B * (t + 1)] = value

    most_in, most_out = QX * SLOTS, QX * SLOTS
    at = lax.broadcasted_iota(jnp.int32, (16, NX), 1)
    z_copies, m_copies = {}, {}
    for chunk, (first, size) in enumerate(CHUNKS):
        for s in range(NQ):
            from_q = (q + NQ - s) % NQ
            if s:
                o_copies[chunk, s].wait_recv()
            else:
                o_copies[chunk, s].wait()
            cp = remote(
                own.at[from_q, first + HALO : first + HALO + size],
                mate.at[from_q, first : first + size],
                m_send.at[chunk, s], m_recv.at[chunk, s], row, twin,
            )
            cp.start()
            m_copies[chunk, s] = cp
        if chunk == 0:
            assemble(edge, 0, HALO, lambda p, t: own[p, 0:HALO, B * t : B * (t + 1)])
            field[HALO - 1 : HALO, :] = edge[0:1, :]
        rows = slice(first, first + size)
        o_rows = slice(first + HALO, first + HALO + size)
        assemble(field, first + HALO, size, lambda p, t: own[p, o_rows, B * t : B * (t + 1)])
        last = 1 if chunk == NC - 1 else 2 + chunk
        after = first + HALO + size
        field[after : after + 1, :] = edge[last : last + 1, :]
        if chunk == 0:
            for cp in loads:
                cp.wait()
        for s in range(NQ):
            c_copies[chunk, s].wait_recv()
            m_copies[chunk, s].wait_recv()
        assemble(
            diff, first, size,
            lambda p, t: (
                mate[p, rows, B * t : B * (t + 1)] - cross[p, rows, B * t : B * (t + 1)]
            ) * sign,
        )
        for r in range(first, first + size, 16):
            r0 = r + HALO
            here_f = field[r0 : r0 + 16, :]
            low = jnp.where(at == 0, 0.0, pltpu.roll(here_f, 1, 1))
            high = jnp.where(at == NX - 1, 0.0, pltpu.roll(here_f, NX - 1, 1))
            grad_z = field[r0 + 1 : r0 + 17, :] - field[r0 - 1 : r0 + 15, :]
            u, v, w = [vel[j, r : r + 16, :].astype(F32) for j in range(3)]
            advection = u * ((high - low) * spacing[...])
            advection += 0.5 * (v * diff[r : r + 16, :]) + 0.5 * (w * grad_z)
            right[r : r + 16, :] = here_f - advection
        end = None
        for k in range(KX):
            across_k = inverse[k].T
            y = jnp.dot(
                right[rows, B * k : B * (k + 1)], across_k, precision=HIGH,
                preferred_element_type=F32,
            )
            if k:
                y = y + (link[k - 1] * across_k[0:1, :]) * end
            if k < KX - 1:
                coef[k : k + 1, :] = link[k] * across_k[B - 1 : B, :]
            end = y[:, B - 1 : B]
            solved[rows, B * k : B * (k + 1)] = y
        head = None
        for k in reversed(range(KX)):
            y = solved[rows, B * k : B * (k + 1)]
            if k < KX - 1:
                y = y + coef[k : k + 1, :] * head
                solved[rows, B * k : B * (k + 1)] = y
            head = y[:, 0:1]
        for p in range(NQ):
            for b in range(tout):
                value = jnp.zeros((size, B), F32)
                for t in quad_tiles(p, most_out):
                    if t % tout == b:
                        value = jnp.where(
                            covers(begins_out, p, t), solved[rows, B * t : B * (t + 1)], value
                        )
                packed[p, rows, B * b : B * (b + 1)] = value
        for s in range(NQ - 1, 0, -1):
            to_q = (q + s) % NQ
            cp = remote(
                packed.at[to_q, rows], rz.at[q, rows],
                z_send.at[chunk, s], z_recv.at[chunk, s], QX * to_q + x, c,
            )
            cp.start()
            z_copies[chunk, s] = cp

    pieces = []
    for i in range(QX):
        at_row = QX * q + (x + i) % QX
        pieces.append(slot_masks(tout, start_at(counts_out, at_row), counts_out[at_row], lane))
    y_copies = []
    for chunk, (first, size) in enumerate(CHUNKS):
        for s in range(NQ):
            from_q = (q + NQ - s) % NQ
            if s:
                z_copies[chunk, s].wait_recv()

            def step(j, carry):
                at_rows = pl.ds(pl.multiple_of(first + 8 * j, 8), 8)
                if s:
                    parts = [rz[from_q, at_rows, B * t : B * (t + 1)] for t in range(tout)]
                else:
                    parts = [packed[q, at_rows, B * t : B * (t + 1)] for t in range(tout)]
                for d in range(QX):
                    value = jnp.zeros((8, B), F32)
                    for t in range(tout):
                        value = jnp.where(pieces[d][t], parts[t], value)
                    piece[d, s, at_rows, :] = value
                return carry

            lax.fori_loop(0, size // 8, step, 0)
            to = pl.multiple_of(ZL * (QX * from_q + x) + first, 8)
            for d in range(QX):
                part, goal = piece.at[d, s, first : first + size], out.at[pl.ds(to, size), :]
                if d:
                    cp = remote(
                        part, goal, y_send.at[chunk, d, s], y_recv.at[chunk, d, s],
                        QX * q + (x + d) % QX, c,
                    )
                else:
                    cp = pltpu.make_async_copy(part, goal, y_local.at[chunk, s])
                cp.start()
                y_copies.append(cp)
    for cp in y_copies:
        cp.wait()
    for chunk in range(NC):
        for s in range(NQ):
            m_copies[chunk, s].wait_send()
            c_copies[chunk, s].wait_send()
            if s:
                o_copies[chunk, s].wait_send()
                z_copies[chunk, s].wait_send()
    for s in range(NQ):
        for cp in x_copies[s][1:]:
            cp.wait_send()


def flow(tin, tout, cid, counts_in, counts_out, link, turned, vel, spacing, inverse):
    dma = pltpu.SemaphoreType.DMA
    vmem = pl.BlockSpec(memory_space=pltpu.VMEM)
    smem = pl.BlockSpec(memory_space=pltpu.SMEM)
    hbm = pl.BlockSpec(memory_space=pl.ANY)
    rows = ZL + HALO
    per = dma((NC, NQ))
    return pl.pallas_call(
        functools.partial(flow_kernel, tin, tout),
        name="flow%d%d" % (tin, tout),
        out_shape=jax.ShapeDtypeStruct((KZ * B, B), F32),
        in_specs=[smem, smem, smem, vmem, hbm, vmem, hbm],
        out_specs=hbm,
        scratch_shapes=[
            pltpu.VMEM((QX, NQ, ZL + 2 * HALO, B), F32),
            pltpu.VMEM((NQ, rows, tin * B), F32),
            pltpu.VMEM((NQ, rows, tin * B), F32),
            pltpu.VMEM((NQ, ZL, tin * B), F32),
            pltpu.VMEM((NQ, ZL, tin * B), F32),
            pltpu.VMEM((3, ZL, NX), jnp.bfloat16),
            pltpu.VMEM((KX, B, B), F32),
            pltpu.VMEM((ZL + 2 * HALO, NX), F32),
            pltpu.VMEM((HALO, NX), F32),
            pltpu.VMEM((ZL, NX), F32),
            pltpu.VMEM((ZL, NX), F32),
            pltpu.VMEM((ZL, NX), F32),
            pltpu.VMEM((KX + 4, B), F32),
            pltpu.VMEM((NQ, ZL, tout * B), F32),
            pltpu.VMEM((NQ, ZL, tout * B), F32),
            pltpu.VMEM((QX, NQ, ZL, B), F32),
            dma((2,)), dma((QX, NQ)), dma((QX, NQ)), dma((NQ,)),
            per, per, dma((NC,)), per, per, per, per, per, per,
            dma((NC, QX, NQ)), dma((NC, QX, NQ)), per,
        ],
        compiler_params=pltpu.CompilerParams(
            collective_id=cid, has_side_effects=True, vmem_limit_bytes=LIMIT
        ),
    )(counts_in, counts_out, link, turned, vel, spacing, inverse)


def last_kernel(counts, link, lines, inverse, out, solved):
    q, x, _ = here()
    back = (B - start_at(counts, QX * q + x) % B) % B
    count = counts[QX * q + x]
    valid = lax.broadcasted_iota(jnp.int32, (SLOTS, B), 0) < count
    end = None
    for k in range(KZ):
        y = jnp.dot(
            inverse[k], lines[B * k : B * (k + 1), :], precision=HIGH,
            preferred_element_type=F32,
        )
        if k:
            y = y + (link[k - 1] * inverse[k, :, 0:1]) * end
        end = y[B - 1 : B, :]
        solved[B * k : B * (k + 1), :] = y
    head = None
    for k in reversed(range(KZ)):
        y = solved[B * k : B * (k + 1), :]
        if k < KZ - 1:
            y = y + (link[k] * inverse[k, :, B - 1 : B]) * head
        head = y[0:1, :]
        turned = pltpu.roll(y, back, 1).T
        out[pl.ds(k, SLOTS, stride=KZ), :] = jnp.where(valid, turned[0:SLOTS, :], 0.0)


def on_device(
    temp_in, velocity, spacing_x, inverse_x, link_x, inverse_z, link_z, counts_in, counts_out
):
    vmem = pl.BlockSpec(memory_space=pltpu.VMEM)
    smem = pl.BlockSpec(memory_space=pltpu.SMEM)
    local = pltpu.CompilerParams(vmem_limit_bytes=LIMIT)
    turned = pl.pallas_call(
        turn_kernel,
        name="turn",
        out_shape=jax.ShapeDtypeStruct((KZ * B + 2 * HALO, B), F32),
        in_specs=[smem, vmem],
        out_specs=vmem,
        compiler_params=local,
    )(counts_in, temp_in.reshape(SLOTS * KZ, B))
    sums = jnp.sum(jnp.stack([counts_in, counts_out]).reshape(2, NQ, QX), axis=2)
    wide = (jnp.max(sums, axis=1) > 2 * B).astype(jnp.int32)
    lines = lax.switch(
        2 * wide[0] + wide[1],
        [
            functools.partial(flow, tin, tout, 1 + i)
            for i, (tin, tout) in enumerate(((2, 2), (2, 3), (3, 2), (3, 3)))
        ],
        counts_in, counts_out, link_x, turned,
        velocity.reshape(3, ZL, NX), spacing_x.reshape(1, NX), inverse_x,
    )
    out = pl.pallas_call(
        last_kernel,
        name="last",
        out_shape=jax.ShapeDtypeStruct((SLOTS * KZ, B), F32),
        in_specs=[smem, smem, vmem, vmem],
        out_specs=vmem,
        scratch_shapes=[pltpu.VMEM((KZ * B, B), F32)],
        compiler_params=local,
    )(counts_out, link_z, lines, inverse_z)
    return out.reshape(SLOTS, 1, KZ * B)


def solution(mesh):
    in_specs = (
        P("row", "col", None),
        P(None, "col", "row", None),
        P(),
        P(),
        P(),
        P(),
        P(),
        P(),
        P(),
    )
    out_specs = P("row", "col", None)
    return jax.shard_map(
        on_device, mesh=mesh, in_specs=in_specs, out_specs=out_specs, check_vma=False
    )
```

```python
import functools
import jax
import jax.numpy as jnp
from jax import lax
from jax.experimental import pallas as pl
from jax.experimental.pallas import tpu as pltpu
from jax.sharding import PartitionSpec as P

MESH = pl.DeviceIdType.MESH
HIGH = lax.Precision.HIGH
B = 128
NQ = 8
QX = 4
ZL = 144
SLOTS = 72
KX = 12
KZ = 36
HALO = 8
QUAD = 192
SPAN = ZL + 2 * HALO
RING = 256
REST = 16
NX = KX * B
CHUNKS = ((0, 48), (48, 48), (96, 48))
NC = len(CHUNKS)
F32 = jnp.float32
LIMIT = 48 * 2**20


def here():
    row = lax.axis_index("row")
    return row // QX, row % QX, lax.axis_index("col")


def starts_of(counts):
    starts, total = [], jnp.int32(0)
    for i in range(NQ * QX):
        starts.append(total)
        total = total + counts[i]
    return starts + [total]


def start_at(counts, row):
    total = jnp.int32(0)
    for i in range(NQ * QX - 1):
        total = total + jnp.where(i < row, counts[i], 0)
    return total


def turn_kernel(counts_in, counts_out, temp, out, pick):
    q, x, _ = here()
    shift = start_at(counts_in, QX * q + x) % B
    starts = starts_of(counts_in)
    drift, most = jnp.int32(0), jnp.int32(0)
    ends = starts_of(counts_out)
    for p in range(NQ):
        drift = jnp.maximum(drift, jnp.abs(starts[QX * p] - QUAD * p))
        most = jnp.maximum(most, ends[QX * (p + 1)] - ends[QX * p])
    pick[0] = jnp.where(drift > B, 2, jnp.where(most > RING, 1, 0))
    pad = jnp.zeros((B - SLOTS, B), F32)
    for k in range(KZ):
        block = temp[pl.ds(k, SLOTS, stride=KZ), :]
        turned = jnp.concatenate([block, pad], axis=0).T
        out[HALO + B * k : HALO + B * (k + 1), :] = pltpu.roll(turned, shift, 1)
    total = KZ * B
    out[0:HALO, :] = out[total : total + HALO, :]
    out[total + HALO : total + 2 * HALO, :] = out[HALO : 2 * HALO, :]


def across(c):
    return jnp.where(c % 2 == 1, (c + 1) % 16, (c + 15) % 16)


def barrier(partners):
    sem = pltpu.get_barrier_semaphore()
    for row, col in partners:
        pl.semaphore_signal(
            sem, inc=1, device_id={"row": row, "col": col}, device_id_type=MESH
        )
    pl.semaphore_wait(sem, len(partners))


def remote(src, dst, send, recv, row, col):
    return pltpu.make_async_remote_copy(
        src_ref=src,
        dst_ref=dst,
        send_sem=send,
        recv_sem=recv,
        device_id={"row": row, "col": col},
        device_id_type=MESH,
    )


ORDER = (4, 3, 5, 2, 6, 1, 7, 0)
LAG = 2


def quad_tiles(q, most):
    low = max(QX * q, NX - most * (NQ - q))
    high = min(most * (q + 1), NX - QX * (NQ - 1 - q))
    return range(low // B, (high - 1) // B + 1)


def slot_masks(tiles, start, count, lane):
    first, shift = start // B, start % B
    masks = []
    for t in range(tiles):
        at_first = first % tiles == t
        at_second = (first + 1) % tiles == t
        low = jnp.where(at_first, shift, 2 * B)
        high = jnp.where(at_first, shift + count, 0)
        wrap = jnp.where(at_second, shift + count - B, 0)
        masks.append(((lane >= low) & (lane < high)) | (lane < wrap))
    return masks


class Layout:
    def __init__(self, per_row, halo):
        self.halo = halo
        self.rows = [size * per_row // 2 for _, size in CHUNKS]
        self.at = [sum(self.rows[:i]) for i in range(NC)]
        self.total = sum(self.rows)

    def own(self, chunk):
        if chunk == 0:
            return pl.ds(0, self.halo + self.rows[0])
        return pl.ds(self.halo + self.at[chunk], self.rows[chunk])

    def inner(self, chunk):
        return pl.ds(self.halo + self.at[chunk], self.rows[chunk])

    def bare(self, chunk):
        return pl.ds(self.at[chunk], self.rows[chunk])


EVEN = Layout(3, HALO)
WIDE = Layout(6, 3 * HALO)


def flow_kernel(
    even, wide_out, counts_in, counts_out, link, turned, vel_hbm, spacing, inv_hbm, out,
    xin, merged, own, cross, mate, away, come, vel, inverse, field, edge, diff, right, solved,
    coef, scale, packed, rz, piece,
    load, x_send, x_recv, x_local, o_send, o_recv, o_local, c_send, c_recv, m_send, m_recv,
    n_send, n_recv, z_send, z_recv, y_send, y_recv, y_local,
):
    lay = EVEN if even else WIDE
    q, x, c = here()
    other, twin = across(c), c + 1 - 2 * (c % 2)
    row = QX * q + x
    loads = [
        pltpu.make_async_copy(vel_hbm, vel, load.at[0]),
        pltpu.make_async_copy(inv_hbm, inverse, load.at[1]),
    ]
    for cp in loads:
        cp.start()
    partners = [(QX * q + (x + s) % QX, c) for s in range(1, QX)]
    partners += [(QX * ((q + s) % NQ) + x, c) for s in range(1, NQ)]
    partners += [(QX * ((q + s) % NQ) + x, other) for s in range(NQ)]
    partners += [(row, twin)]
    barrier(partners)

    def source(to_q, to_x):
        start = pl.multiple_of(QX * ZL * to_q + ZL * to_x, 8)
        return turned.at[pl.ds(start, SPAN), :]

    x_copies = {}
    for s in ORDER:
        to_q = (q + s) % NQ
        local = pltpu.make_async_copy(source(to_q, x), xin.at[x, s], x_local.at[s])
        local.start()
        x_copies[s] = [local]
        for d in range(1, QX):
            to_x = (x + d) % QX
            cp = remote(
                source(to_q, to_x), xin.at[x, s], x_send.at[d, s], x_recv.at[d, s],
                QX * q + to_x, c,
            )
            cp.start()
            x_copies[s].append(cp)

    lane = lax.broadcasted_iota(jnp.int32, (8, B), 1)
    sub = lax.broadcasted_iota(jnp.int32, (8, B), 0)
    edge_rows = [-1, ZL] + [first + size for first, size in CHUNKS[:-1]]
    quad_first = start_at(counts_in, QX * q)
    firsts = [quad_first]
    for i in range(QX):
        firsts.append(firsts[-1] + counts_in[QX * q + i])

    def choose(masks, parts):
        value = jnp.zeros((8, B), F32)
        for mask, part in zip(masks, parts):
            value = jnp.where(mask, part, value)
        return value

    def arrived(s):
        x_copies[s][0].wait()
        for cp in x_copies[s][1:]:
            cp.wait_recv()

    def edge_parts(s, rows, read):
        value = jnp.zeros((8, B), F32)
        for n, z in rows:
            value = jnp.where(sub == n, read(z), value)
        return value

    n_copies = {}
    if even:
        odd = q % 2
        full_at = QUAD * q + (B // 2) * odd
        half_at = QUAD * q + B - (3 * B // 2) * odd
        natural = (lane < B // 2) == (jnp.zeros((8, B), jnp.int32) + odd == 0)

        def inside(place):
            return [(place >= firsts[i]) & (place < firsts[i + 1]) for i in range(QX)]

        def quad_masks(place):
            return inside(place) + [place < firsts[0], place >= firsts[QX]]

        full_masks, half_masks = quad_masks(lane + full_at), quad_masks(lane + half_at)
        window_masks = []
        for base in (QUAD * (q + 1), QUAD * q - B):
            turn = (base + B) % B
            window_masks.append(inside(lane + (base - turn) + jnp.where(lane < turn, B, 0)))

        def prepare(s):
            arrived(s)

            def step(j, carry):
                rows = pl.ds(pl.multiple_of(8 * j, 8), 8)
                parts = [xin[i, s, rows, :] for i in range(QX)]
                for side in range(2):
                    away[side, s, rows, :] = choose(window_masks[side], parts)
                return carry

            lax.fori_loop(0, SPAN // 8, step, 0)
            to_q = (q + s) % NQ
            for side, (inner, to) in enumerate(((q < NQ - 1, q + 1), (q > 0, q - 1))):
                to = (to + NQ) % NQ
                cp = remote(
                    away.at[side, s], come.at[side, to_q],
                    n_send.at[side, to_q], n_recv.at[side, to_q], QX * to + x, c,
                )
                n_copies[side, s] = cp
                pl.when(inner)(cp.start)

        def merge(s):
            to_q = (q + s) % NQ
            pl.when(q > 0)(n_copies[0, s].wait_recv)
            pl.when(q < NQ - 1)(n_copies[1, s].wait_recv)

            def parts_at(rows):
                parts = [xin[i, s, rows, :] for i in range(QX)]
                return parts + [come[side, to_q, rows, :] for side in range(2)]

            for chunk, (first, size) in enumerate(CHUNKS):
                base = lay.halo + lay.at[chunk]

                def step(j, carry):
                    r = pl.multiple_of(8 * j, 8)
                    halves = []
                    for up in (0, size // 2):
                        parts = parts_at(pl.ds(HALO + first + up + r, 8))
                        merged[s, pl.ds(base + up + r, 8), :] = choose(full_masks, parts)
                        halves.append(choose(half_masks, parts))
                    merged[s, pl.ds(base + size + r, 8), :] = jnp.where(
                        natural, halves[0], pltpu.roll(halves[1], B // 2, 1)
                    )
                    return carry

                lax.fori_loop(0, size // 16, step, 0)
            parts = []
            for rows in (
                [lambda z, i=i: xin[i, s, HALO + z : HALO + z + 1, :] for i in range(QX)]
                + [lambda z, i=i: come[i, to_q, HALO + z : HALO + z + 1, :] for i in range(2)]
            ):
                pairs = [(n, z) for n, z in enumerate(edge_rows)]
                parts.append(edge_parts(s, pairs + [(4 + n, z) for n, z in pairs], rows))
            merged[s, 0:HALO, :] = jnp.where(
                sub < 4, choose(full_masks, parts), choose(half_masks, parts)
            )

    else:
        takes = [
            slot_masks(3, firsts[i], firsts[i + 1] - firsts[i], lane) for i in range(QX)
        ]

        def prepare(s):
            arrived(s)

        def merge(s):
            for chunk, (first, size) in enumerate(CHUNKS):
                base = lay.halo + lay.at[chunk]

                def step(j, carry):
                    r = pl.multiple_of(8 * j, 8)
                    parts = [xin[i, s, pl.ds(HALO + first + r, 8), :] for i in range(QX)]
                    for t in range(3):
                        merged[s, pl.ds(base + t * size + r, 8), :] = choose(
                            [takes[i][t] for i in range(QX)], parts
                        )
                    return carry

                lax.fori_loop(0, size // 8, step, 0)
            parts = [
                edge_parts(
                    s, list(enumerate(edge_rows)),
                    lambda z, i=i: xin[i, s, HALO + z : HALO + z + 1, :],
                )
                for i in range(QX)
            ]
            for t in range(3):
                merged[s, HALO * t : HALO * (t + 1), :] = choose(
                    [takes[i][t] for i in range(QX)], parts
                )

    def send_rows(s, chunk):
        to_q = (q + s) % NQ
        o_src, o_dst = merged.at[s, lay.own(chunk)], own.at[q, lay.own(chunk)]
        if s:
            o_copy = remote(
                o_src, o_dst, o_send.at[chunk, s], o_recv.at[chunk, s], QX * to_q + x, c
            )
        else:
            o_copy = pltpu.make_async_copy(o_src, o_dst, o_local.at[chunk])
        o_copy.start()
        c_copy = remote(
            merged.at[s, lay.inner(chunk)], cross.at[q, lay.bare(chunk)],
            c_send.at[chunk, s], c_recv.at[chunk, s], QX * to_q + x, other,
        )
        c_copy.start()
        return o_copy, c_copy

    o_copies, c_copies = {}, {}
    lag = LAG if even else 0
    for n in range(NQ + lag):
        if n < NQ:
            prepare(ORDER[n])
        if n >= lag:
            s = ORDER[n - lag]
            merge(s)
            o_copies[0, s], c_copies[0, s] = send_rows(s, 0)
    for chunk in range(1, NC):
        for s in ORDER:
            o_copies[chunk, s], c_copies[chunk, s] = send_rows(s, chunk)

    line = lax.broadcasted_iota(jnp.int32, (1, B), 1)
    begins_in = starts_of(counts_in)[::QX]
    begins_out = starts_of(counts_out)[::QX]
    sign = jnp.where(c % 2 == 0, F32(1), F32(-1))
    most = QX * SLOTS

    def covers(low, high, t):
        return (line >= low - B * t) & (line < high - B * t)

    def assemble(dst, to, size, read):
        if not even:
            for t in range(KX):
                value = jnp.zeros((size, B), F32)
                for p in range(NQ):
                    if t in quad_tiles(p, most):
                        mask = covers(begins_in[p], begins_in[p + 1], t)
                        value = jnp.where(mask, read(p, size * (t % 3), size), value)
                dst[to : to + size, B * t : B * (t + 1)] = value
            return
        h = size // 2
        for m in range(NQ // 2):
            lo, hi = 2 * m, 2 * m + 1
            cols = [slice(B * (3 * m + t), B * (3 * m + t + 1)) for t in range(3)]
            dst[to : to + size, cols[0]] = read(lo, 0, size)
            dst[to : to + size, cols[2]] = read(hi, 0, size)
            a, b = read(lo, size, h), read(hi, size, h)
            dst[to : to + h, cols[1]] = jnp.where(line < B // 2, a, b)
            dst[to + h : to + size, cols[1]] = pltpu.roll(
                jnp.where(line < B // 2, b, a), B // 2, 1
            )

    def assemble_edge():
        if not even:
            assemble(edge, 0, HALO, lambda p, r, n: own[p, r : r + n, :])
            return
        for m in range(NQ // 2):
            lo, hi = own[2 * m, 0:HALO, :], own[2 * m + 1, 0:HALO, :]
            at = 3 * m * B
            edge[0:4, at : at + B] = lo[0:4]
            edge[0:4, at + B : at + 2 * B] = jnp.where(line < B // 2, lo, hi)[4:8]
            edge[0:4, at + 2 * B : at + 3 * B] = hi[0:4]

    for t in range(KX):
        scale[0:1, B * t : B * (t + 1)] = spacing[t : t + 1, :]
    at = lax.broadcasted_iota(jnp.int32, (16, NX), 1)
    per_out = 2 * 48 + (REST if wide_out else 0)
    group = lane // 32
    group16 = lax.broadcasted_iota(jnp.int32, (REST, B), 1) // 32
    z_copies, m_copies = {}, {}
    for chunk, (first, size) in enumerate(CHUNKS):
        for s in range(NQ):
            from_q = (q + NQ - s) % NQ
            if s:
                o_copies[chunk, s].wait_recv()
            else:
                o_copies[chunk, s].wait()
            cp = remote(
                own.at[from_q, lay.inner(chunk)], mate.at[from_q, lay.bare(chunk)],
                m_send.at[chunk, s], m_recv.at[chunk, s], row, twin,
            )
            cp.start()
            m_copies[chunk, s] = cp
        if chunk == 0:
            assemble_edge()
            field[HALO - 1 : HALO, :] = edge[0:1, :]
        rows = slice(first, first + size)
        o_at, c_at = lay.halo + lay.at[chunk], lay.at[chunk]
        assemble(
            field, first + HALO, size, lambda p, r, n: own[p, o_at + r : o_at + r + n, :]
        )
        last = 1 if chunk == NC - 1 else 2 + chunk
        after = first + HALO + size
        field[after : after + 1, :] = edge[last : last + 1, :]
        if chunk == 0:
            for cp in loads:
                cp.wait()
        for s in range(NQ):
            c_copies[chunk, s].wait_recv()
            m_copies[chunk, s].wait_recv()
        assemble(
            diff, first, size,
            lambda p, r, n: (
                mate[p, c_at + r : c_at + r + n, :] - cross[p, c_at + r : c_at + r + n, :]
            ) * sign,
        )
        for r in range(first, first + size, 16):
            r0 = r + HALO
            here_f = field[r0 : r0 + 16, :]
            low = jnp.where(at == 0, 0.0, pltpu.roll(here_f, 1, 1))
            high = jnp.where(at == NX - 1, 0.0, pltpu.roll(here_f, NX - 1, 1))
            grad_z = field[r0 + 1 : r0 + 17, :] - field[r0 - 1 : r0 + 15, :]
            u, v, w = [vel[j, r : r + 16, :].astype(F32) for j in range(3)]
            advection = u * ((high - low) * scale[0:1, :])
            advection += 0.5 * (v * diff[r : r + 16, :]) + 0.5 * (w * grad_z)
            right[r : r + 16, :] = here_f - advection
        end = None
        for k in range(KX):
            across_k = inverse[k].T
            y = jnp.dot(
                right[rows, B * k : B * (k + 1)], across_k, precision=HIGH,
                preferred_element_type=F32,
            )
            if k:
                y = y + (link[k - 1] * across_k[0:1, :]) * end
            if k < KX - 1:
                coef[k : k + 1, :] = link[k] * across_k[B - 1 : B, :]
            end = y[:, B - 1 : B]
            solved[rows, B * k : B * (k + 1)] = y
        head = None
        for k in reversed(range(KX)):
            y = solved[rows, B * k : B * (k + 1)]
            if k < KX - 1:
                y = y + coef[k : k + 1, :] * head
                solved[rows, B * k : B * (k + 1)] = y
            head = y[:, 0:1]
        out_at = per_out * chunk
        for p in range(NQ):
            limit = jnp.minimum(begins_out[p] + RING, begins_out[p + 1])
            values = [jnp.zeros((size, B), F32) for _ in range(2)]
            rest = jnp.zeros((size, B), F32)
            for t in quad_tiles(p, most):
                tile = solved[rows, B * t : B * (t + 1)]
                values[t % 2] = jnp.where(covers(begins_out[p], limit, t), tile, values[t % 2])
                if wide_out:
                    rest = jnp.where(covers(limit, begins_out[p + 1], t), tile, rest)
            for b in range(2):
                packed[p, out_at + size * b : out_at + size * (b + 1), :] = values[b]
            if wide_out:
                rest = rest + pltpu.roll(rest, B // 2, 1)
                rest = rest + pltpu.roll(rest, B // 4, 1)
                tight = rest[2 * REST : 3 * REST]
                for g in (1, 0):
                    tight = jnp.where(group16 == g, rest[REST * g : REST * (g + 1)], tight)
                packed[p, out_at + 2 * size : out_at + 2 * size + REST, :] = tight
        for s in range(NQ - 1, 0, -1):
            to_q = (q + s) % NQ
            cp = remote(
                packed.at[to_q, pl.ds(out_at, per_out)], rz.at[q, pl.ds(out_at, per_out)],
                z_send.at[chunk, s], z_recv.at[chunk, s], QX * to_q + x, c,
            )
            cp.start()
            z_copies[chunk, s] = cp

    pieces, rests = [], []
    limit = start_at(counts_out, QX * q) + RING
    for i in range(QX):
        at_row = QX * q + (x + i) % QX
        begin, count = start_at(counts_out, at_row), counts_out[at_row]
        inner = jnp.minimum(jnp.maximum(limit - begin, 0), count)
        pieces.append(slot_masks(2, begin, inner, lane))
        rests.append(slot_masks(1, begin + inner, count - inner, lane)[0])
    y_copies = []
    for chunk, (first, size) in enumerate(CHUNKS):
        out_at = per_out * chunk
        for s in range(NQ):
            from_q = (q + NQ - s) % NQ
            if s:
                z_copies[chunk, s].wait_recv()

            def step(j, carry):
                r = pl.multiple_of(8 * j, 8)

                def read(to):
                    if s:
                        return rz[from_q, pl.ds(out_at + to + r, 8), :]
                    return packed[q, pl.ds(out_at + to + r, 8), :]

                for g in range(size // REST):
                    parts = [read(REST * g), read(size + REST * g)]
                    if wide_out:
                        rest = jnp.where(group == g, read(2 * size), 0.0)
                        rest = rest + pltpu.roll(rest, B // 2, 1)
                        parts.append(rest + pltpu.roll(rest, B // 4, 1))
                    for d in range(QX):
                        masks = pieces[d] + ([rests[d]] if wide_out else [])
                        piece[d, s, pl.ds(first + REST * g + r, 8), :] = choose(masks, parts)
                return carry

            lax.fori_loop(0, REST // 8, step, 0)
            to = pl.multiple_of(ZL * (QX * from_q + x) + first, 8)
            for d in range(QX):
                part, goal = piece.at[d, s, pl.ds(first, size)], out.at[pl.ds(to, size), :]
                if d:
                    cp = remote(
                        part, goal, y_send.at[chunk, d, s], y_recv.at[chunk, d, s],
                        QX * q + (x + d) % QX, c,
                    )
                else:
                    cp = pltpu.make_async_copy(part, goal, y_local.at[chunk, s])
                cp.start()
                y_copies.append(cp)
    for cp in y_copies:
        cp.wait()
    for chunk in range(NC):
        for s in range(NQ):
            m_copies[chunk, s].wait_send()
            c_copies[chunk, s].wait_send()
            if s:
                o_copies[chunk, s].wait_send()
                z_copies[chunk, s].wait_send()
    for s in range(NQ):
        for cp in x_copies[s][1:]:
            cp.wait_send()
        if even:
            pl.when(q < NQ - 1)(n_copies[0, s].wait_send)
            pl.when(q > 0)(n_copies[1, s].wait_send)


def flow(even, wide_out, cid, counts_in, counts_out, link, turned, vel, spacing, inverse):
    dma = pltpu.SemaphoreType.DMA
    vmem = pl.BlockSpec(memory_space=pltpu.VMEM)
    smem = pl.BlockSpec(memory_space=pltpu.SMEM)
    hbm = pl.BlockSpec(memory_space=pl.ANY)
    per = dma((NC, NQ))
    lay = EVEN if even else WIDE
    per_out = NC * (2 * 48 + (REST if wide_out else 0))
    return pl.pallas_call(
        functools.partial(flow_kernel, even, wide_out),
        name="flow%d%d" % (even, wide_out),
        out_shape=jax.ShapeDtypeStruct((KZ * B, B), F32),
        in_specs=[smem, smem, smem, vmem, hbm, vmem, hbm],
        out_specs=hbm,
        scratch_shapes=[
            pltpu.VMEM((QX, NQ, SPAN, B), F32),
            pltpu.VMEM((NQ, lay.halo + lay.total, B), F32),
            pltpu.VMEM((NQ, lay.halo + lay.total, B), F32),
            pltpu.VMEM((NQ, lay.total, B), F32),
            pltpu.VMEM((NQ, lay.total, B), F32),
            pltpu.VMEM((2, NQ, SPAN, B), F32),
            pltpu.VMEM((2, NQ, SPAN, B), F32),
            pltpu.VMEM((3, ZL, NX), jnp.bfloat16),
            pltpu.VMEM((KX, B, B), F32),
            pltpu.VMEM((SPAN, NX), F32),
            pltpu.VMEM((HALO, NX), F32),
            pltpu.VMEM((ZL, NX), F32),
            pltpu.VMEM((ZL, NX), F32),
            pltpu.VMEM((ZL, NX), F32),
            pltpu.VMEM((KX + 4, B), F32),
            pltpu.VMEM((HALO, NX), F32),
            pltpu.VMEM((NQ, per_out, B), F32),
            pltpu.VMEM((NQ, per_out, B), F32),
            pltpu.VMEM((QX, NQ, ZL, B), F32),
            dma((2,)), dma((QX, NQ)), dma((QX, NQ)), dma((NQ,)),
            per, per, dma((NC,)), per, per, per, per,
            dma((2, NQ)), dma((2, NQ)), per, per,
            dma((NC, QX, NQ)), dma((NC, QX, NQ)), per,
        ],
        compiler_params=pltpu.CompilerParams(
            collective_id=cid, has_side_effects=True, vmem_limit_bytes=LIMIT
        ),
    )(counts_in, counts_out, link, turned, vel, spacing, inverse)


def last_kernel(counts, link, lines, inverse, out, solved):
    q, x, _ = here()
    back = (B - start_at(counts, QX * q + x) % B) % B
    count = counts[QX * q + x]
    valid = lax.broadcasted_iota(jnp.int32, (SLOTS, B), 0) < count
    end = None
    for k in range(KZ):
        y = jnp.dot(
            inverse[k], lines[B * k : B * (k + 1), :], precision=HIGH,
            preferred_element_type=F32,
        )
        if k:
            y = y + (link[k - 1] * inverse[k, :, 0:1]) * end
        end = y[B - 1 : B, :]
        solved[B * k : B * (k + 1), :] = y
    head = None
    for k in reversed(range(KZ)):
        y = solved[B * k : B * (k + 1), :]
        if k < KZ - 1:
            y = y + (link[k] * inverse[k, :, B - 1 : B]) * head
        head = y[0:1, :]
        turned = pltpu.roll(y, back, 1).T
        out[pl.ds(k, SLOTS, stride=KZ), :] = jnp.where(valid, turned[0:SLOTS, :], 0.0)


def on_device(
    temp_in, velocity, spacing_x, inverse_x, link_x, inverse_z, link_z, counts_in, counts_out
):
    vmem = pl.BlockSpec(memory_space=pltpu.VMEM)
    smem = pl.BlockSpec(memory_space=pltpu.SMEM)
    local = pltpu.CompilerParams(vmem_limit_bytes=LIMIT)
    turned, pick = pl.pallas_call(
        turn_kernel,
        name="turn",
        out_shape=(
            jax.ShapeDtypeStruct((KZ * B + 2 * HALO, B), F32),
            jax.ShapeDtypeStruct((1,), jnp.int32),
        ),
        in_specs=[smem, smem, vmem],
        out_specs=(vmem, smem),
        compiler_params=local,
    )(counts_in, counts_out, temp_in.reshape(SLOTS * KZ, B))
    lines = lax.switch(
        pick[0],
        [
            functools.partial(flow, even, wide_out, 1 + i)
            for i, (even, wide_out) in enumerate(((1, 0), (1, 1), (0, 1)))
        ],
        counts_in, counts_out, link_x, turned,
        velocity.reshape(3, ZL, NX), spacing_x.reshape(KX, B), inverse_x,
    )
    out = pl.pallas_call(
        last_kernel,
        name="last",
        out_shape=jax.ShapeDtypeStruct((SLOTS * KZ, B), F32),
        in_specs=[smem, smem, vmem, vmem],
        out_specs=vmem,
        scratch_shapes=[pltpu.VMEM((KZ * B, B), F32)],
        compiler_params=local,
    )(counts_out, link_z, lines, inverse_z)
    return out.reshape(SLOTS, 1, KZ * B)


def solution(mesh):
    in_specs = (
        P("row", "col", None),
        P(None, "col", "row", None),
        P(),
        P(),
        P(),
        P(),
        P(),
        P(),
        P(),
    )
    out_specs = P("row", "col", None)
    return jax.shard_map(
        on_device, mesh=mesh, in_specs=in_specs, out_specs=out_specs, check_vma=False
    )
```

```python
import functools
import jax
import jax.numpy as jnp
from jax import lax
from jax.experimental import pallas as pl
from jax.experimental.pallas import tpu as pltpu
from jax.sharding import PartitionSpec as P

MESH = pl.DeviceIdType.MESH
HIGH = lax.Precision.HIGH
B = 128
NQ = 8
QX = 4
ZL = 144
SLOTS = 72
KX = 12
KZ = 36
HALO = 8
QUAD = 192
SPAN = ZL + 2 * HALO
RING = 256
REST = 16
PARTS = 6
NX = KX * B
CHUNKS = ((0, 64), (64, 48), (112, 32))
STEPS = ((0, 48), (48, 48), (96, 48))
NC = len(CHUNKS)
MAIN = 2 * HALO
F32 = jnp.float32
LIMIT = 48 * 2**20


def here():
    row = lax.axis_index("row")
    return row // QX, row % QX, lax.axis_index("col")


def starts_of(counts):
    starts, total = [], jnp.int32(0)
    for i in range(NQ * QX):
        starts.append(total)
        total = total + counts[i]
    return starts + [total]


def start_at(counts, row):
    total = jnp.int32(0)
    for i in range(NQ * QX - 1):
        total = total + jnp.where(i < row, counts[i], 0)
    return total


def pick_kernel(counts_in, counts_out, pick):
    starts, ends = starts_of(counts_in), starts_of(counts_out)
    drift, most = jnp.int32(0), jnp.int32(0)
    for p in range(NQ):
        drift = jnp.maximum(drift, jnp.abs(starts[QX * p] - QUAD * p))
        most = jnp.maximum(most, ends[QX * (p + 1)] - ends[QX * p])
    pick[0] = jnp.where(drift > B, 2, jnp.where(most > RING, 1, 0))


def across(c):
    return jnp.where(c % 2 == 1, (c + 1) % 16, (c + 15) % 16)


def barrier(partners):
    sem = pltpu.get_barrier_semaphore()
    for row, col in partners:
        pl.semaphore_signal(
            sem, inc=1, device_id={"row": row, "col": col}, device_id_type=MESH
        )
    return lambda: pl.semaphore_wait(sem, len(partners))


def remote(src, dst, send, recv, row, col):
    return pltpu.make_async_remote_copy(
        src_ref=src,
        dst_ref=dst,
        send_sem=send,
        recv_sem=recv,
        device_id={"row": row, "col": col},
        device_id_type=MESH,
    )


ORDER = (4, 3, 5, 2, 6, 1, 7, 0)
LAG = 4


def quad_tiles(q, most):
    low = max(QX * q, NX - most * (NQ - q))
    high = min(most * (q + 1), NX - QX * (NQ - 1 - q))
    return range(low // B, (high - 1) // B + 1)


def slot_masks(tiles, start, count, lane):
    first, shift = start // B, start % B
    masks = []
    for t in range(tiles):
        at_first = first % tiles == t
        at_second = (first + 1) % tiles == t
        low = jnp.where(at_first, shift, 2 * B)
        high = jnp.where(at_first, shift + count, 0)
        wrap = jnp.where(at_second, shift + count - B, 0)
        masks.append(((lane >= low) & (lane < high)) | (lane < wrap))
    return masks


class Layout:
    def __init__(self, per_two, rest, halo):
        self.halo = halo
        self.rows = [size * per_two // 2 + rest for _, size in CHUNKS]
        self.at = [sum(self.rows[:i]) for i in range(NC)]
        self.total = sum(self.rows)

    def own(self, chunk):
        if chunk == 0:
            return pl.ds(0, self.halo + self.rows[0])
        return self.inner(chunk)

    def inner(self, chunk):
        return pl.ds(self.halo + self.at[chunk], self.rows[chunk])

    def bare(self, chunk):
        return pl.ds(self.at[chunk], self.rows[chunk])


EVEN = Layout(3, 0, HALO)
WIDE = Layout(4, REST, 3 * HALO)


def flow_kernel(
    even, wide_out, counts_in, counts_out, link, temp_hbm, vel_hbm, spacing, inv_hbm, out,
    temp, doubled, turned, xin, merged, own, cross, mate, away, come, vel, inverse, field, edge, diff, right, solved,
    coef, scale, packed, rz, piece,
    load, x_send, x_recv, x_local, o_send, o_recv, o_local, c_send, c_recv, m_send, m_recv,
    n_send, n_recv, z_send, z_recv, y_send, y_recv, y_local,
):
    lay = EVEN if even else WIDE
    q, x, c = here()
    other, twin = across(c), c + 1 - 2 * (c % 2)
    row = QX * q + x
    loads = [
        pltpu.make_async_copy(temp_hbm, temp, load.at[0]),
        pltpu.make_async_copy(vel_hbm, vel, load.at[1]),
        pltpu.make_async_copy(inv_hbm, inverse, load.at[2]),
    ]
    for cp in loads:
        cp.start()
    partners = [(QX * q + (x + s) % QX, c) for s in range(1, QX)]
    partners += [(QX * ((q + s) % NQ) + x, c) for s in range(1, NQ)]
    partners += [(QX * ((q + s) % NQ) + x, other) for s in range(NQ)]
    partners += [(row, twin)]
    ready = barrier(partners)
    loads[0].wait()
    back = B - start_at(counts_in, row) % B
    for j in range(2):
        doubled[j, SLOTS:B, :] = jnp.zeros((B - SLOTS, B), F32)
        doubled[j, B + SLOTS : 2 * B, :] = jnp.zeros((B - SLOTS, B), F32)
    for k in range(KZ):
        block, j = temp[pl.ds(k, SLOTS, stride=KZ), :], k % 2
        doubled[j, 0:SLOTS, :] = block
        doubled[j, B : B + SLOTS, :] = block
        turned[HALO + B * k : HALO + B * (k + 1), :] = doubled[j, pl.ds(back, B), :].T
    total = KZ * B
    turned[0:HALO, :] = turned[total : total + HALO, :]
    turned[total + HALO : total + 2 * HALO, :] = turned[HALO : 2 * HALO, :]
    ready()

    def parts_of(to_q, to_x, chunk):
        start = pl.multiple_of(QX * ZL * to_q + ZL * to_x, 8)
        first, size = CHUNKS[chunk]
        if chunk:
            return [(start + HALO + first, MAIN + first, size)]
        return [(start, HALO, HALO + size), (start + HALO + ZL, 0, HALO)]

    x_copies = {}
    for chunk in range(NC):
        for s in ORDER:
            to_q = (q + s) % NQ
            copies = []
            for d in range(QX):
                to_x = (x + d) % QX
                for n, (at_row, to_row, size) in enumerate(parts_of(to_q, to_x, chunk)):
                    src = turned.at[pl.ds(at_row, size), :]
                    dst = xin.at[x, s, pl.ds(to_row, size), :]
                    sem = chunk + NC * n
                    if d:
                        cp = remote(
                            src, dst, x_send.at[sem, d, s], x_recv.at[sem, d, s],
                            QX * q + to_x, c,
                        )
                    else:
                        cp = pltpu.make_async_copy(src, dst, x_local.at[sem, s])
                    cp.start()
                    copies.append((d, cp))
            x_copies[chunk, s] = copies

    lane = lax.broadcasted_iota(jnp.int32, (8, B), 1)
    sub = lax.broadcasted_iota(jnp.int32, (8, B), 0)
    group = lane // 32
    firsts = [start_at(counts_in, QX * q)]
    for i in range(QX):
        firsts.append(firsts[-1] + counts_in[QX * q + i])

    def choose(masks, parts):
        value = jnp.zeros((8, B), F32)
        for mask, part in zip(masks, parts):
            value = jnp.where(mask, part, value)
        return value

    def fold(value):
        value = value + pltpu.roll(value, B // 2, 1)
        return value + pltpu.roll(value, B // 4, 1)

    def arrived(chunk, s):
        for d, cp in x_copies[chunk, s]:
            if d:
                cp.wait_recv()
            else:
                cp.wait()

    def edge_tile(read):
        low, high = read(MAIN - 1), read(0)
        return jnp.where(sub % 4 == 0, low, high)

    n_copies = {}
    if even:
        odd = q % 2
        full_at = QUAD * q + (B // 2) * odd
        half_at = QUAD * q + B - (3 * B // 2) * odd
        natural = (lane < B // 2) == (jnp.zeros((8, B), jnp.int32) + odd == 0)

        def inside(place):
            return [(place >= firsts[i]) & (place < firsts[i + 1]) for i in range(QX)]

        def quad_masks(place):
            return inside(place) + [place < firsts[0], place >= firsts[QX]]

        full_masks, half_masks = quad_masks(lane + full_at), quad_masks(lane + half_at)
        window_masks = []
        for base in (QUAD * (q + 1), QUAD * q - B):
            turn = (base + B) % B
            window_masks.append(inside(lane + (base - turn) + jnp.where(lane < turn, B, 0)))

        def prepare(chunk, s):
            arrived(chunk, s)
            first, size = CHUNKS[chunk]
            low = 0 if chunk == 0 else MAIN + first
            span = MAIN + first + size - low

            def step(j, carry):
                rows = pl.ds(pl.multiple_of(low + 8 * j, 8), 8)
                parts = [xin[i, s, rows, :] for i in range(QX)]
                for side in range(2):
                    away[side, s, rows, :] = choose(window_masks[side], parts)
                return carry

            lax.fori_loop(0, span // 8, step, 0)
            to_q = (q + s) % NQ
            for side, (inner, to) in enumerate(((q < NQ - 1, q + 1), (q > 0, q - 1))):
                to = (to + NQ) % NQ
                cp = remote(
                    away.at[side, s, pl.ds(low, span), :],
                    come.at[side, to_q, pl.ds(low, span), :],
                    n_send.at[side, chunk, to_q], n_recv.at[side, chunk, to_q],
                    QX * to + x, c,
                )
                n_copies[side, chunk, s] = cp
                pl.when(inner)(cp.start)

        def merge(chunk, s):
            to_q = (q + s) % NQ
            pl.when(q > 0)(n_copies[0, chunk, s].wait_recv)
            pl.when(q < NQ - 1)(n_copies[1, chunk, s].wait_recv)

            def parts_at(rows):
                parts = [xin[i, s, rows, :] for i in range(QX)]
                return parts + [come[side, to_q, rows, :] for side in range(2)]

            first, size = CHUNKS[chunk]
            base = lay.halo + lay.at[chunk]

            def step(j, carry):
                r = pl.multiple_of(8 * j, 8)
                halves = []
                for up in (0, size // 2):
                    parts = parts_at(pl.ds(MAIN + first + up + r, 8))
                    merged[s, pl.ds(base + up + r, 8), :] = choose(full_masks, parts)
                    halves.append(choose(half_masks, parts))
                merged[s, pl.ds(base + size + r, 8), :] = jnp.where(
                    natural, halves[0], pltpu.roll(halves[1], B // 2, 1)
                )
                return carry

            lax.fori_loop(0, size // 16, step, 0)
            if chunk == 0:
                parts = [
                    edge_tile(lambda r, i=i: xin[i, s, r : r + 1, :]) for i in range(QX)
                ]
                parts += [
                    edge_tile(lambda r, i=i: come[i, to_q, r : r + 1, :]) for i in range(2)
                ]
                merged[s, 0:HALO, :] = jnp.where(
                    sub < 4, choose(full_masks, parts), choose(half_masks, parts)
                )

    else:
        limit_in = firsts[0] + RING
        takes, rest_takes = [], []
        for i in range(QX):
            count = firsts[i + 1] - firsts[i]
            inner = jnp.minimum(jnp.maximum(limit_in - firsts[i], 0), count)
            takes.append(slot_masks(2, firsts[i], inner, lane))
            rest_takes.append(slot_masks(1, firsts[i] + inner, count - inner, lane)[0])

        def prepare(chunk, s):
            arrived(chunk, s)

        def merge(chunk, s):
            first, size = CHUNKS[chunk]
            base = lay.halo + lay.at[chunk]

            def step(j, carry):
                r = pl.multiple_of(8 * j, 8)
                tight = jnp.zeros((8, B), F32)
                for g in range(size // REST):
                    at_row = REST * g + r
                    parts = [xin[i, s, pl.ds(MAIN + first + at_row, 8), :] for i in range(QX)]
                    for t in range(2):
                        merged[s, pl.ds(base + t * size + at_row, 8), :] = choose(
                            [takes[i][t] for i in range(QX)], parts
                        )
                    tight = jnp.where(group == g, fold(choose(rest_takes, parts)), tight)
                merged[s, pl.ds(base + 2 * size + r, 8), :] = tight
                return carry

            lax.fori_loop(0, REST // 8, step, 0)
            if chunk == 0:
                parts = [
                    edge_tile(lambda r, i=i: xin[i, s, r : r + 1, :]) for i in range(QX)
                ]
                for t in range(2):
                    merged[s, HALO * t : HALO * (t + 1), :] = choose(
                        [takes[i][t] for i in range(QX)], parts
                    )
                merged[s, 2 * HALO : 3 * HALO, :] = fold(choose(rest_takes, parts))

    def send_rows(s, chunk):
        to_q = (q + s) % NQ
        o_src, o_dst = merged.at[s, lay.own(chunk)], own.at[q, lay.own(chunk)]
        if s:
            o_copy = remote(
                o_src, o_dst, o_send.at[chunk, s], o_recv.at[chunk, s], QX * to_q + x, c
            )
        else:
            o_copy = pltpu.make_async_copy(o_src, o_dst, o_local.at[chunk])
        o_copy.start()
        c_copy = remote(
            merged.at[s, lay.inner(chunk)], cross.at[q, lay.bare(chunk)],
            c_send.at[chunk, s], c_recv.at[chunk, s], QX * to_q + x, other,
        )
        c_copy.start()
        return o_copy, c_copy

    o_copies, c_copies = {}, {}
    lag = LAG if even else 0
    todo = [(chunk, s) for chunk in range(NC) for s in ORDER]
    for n in range(len(todo) + lag):
        if n < len(todo):
            prepare(*todo[n])
        if n >= lag:
            chunk, s = todo[n - lag]
            merge(chunk, s)
            o_copies[chunk, s], c_copies[chunk, s] = send_rows(s, chunk)

    line = lax.broadcasted_iota(jnp.int32, (1, B), 1)
    begins_in = starts_of(counts_in)[::QX]
    begins_out = starts_of(counts_out)[::QX]
    sign = jnp.where(c % 2 == 0, F32(1), F32(-1))
    most = QX * SLOTS

    def covers(low, high, t):
        return (line >= low - B * t) & (line < high - B * t)

    def assemble(dst, to, size, read):
        if not even:
            rests = []
            for p in range(NQ):
                if size == HALO:
                    rests.append(read(p, 2 * size, HALO))
                    continue
                tight = read(p, 2 * size, REST)
                groups = [
                    fold(jnp.where(group16 == g, tight, 0.0)) for g in range(size // REST)
                ]
                rests.append(jnp.concatenate(groups, axis=0))
            for t in range(KX):
                value = jnp.zeros((size, B), F32)
                for p in range(NQ):
                    if t in quad_tiles(p, most):
                        limit = jnp.minimum(begins_in[p] + RING, begins_in[p + 1])
                        part = read(p, size * (t % 2), size)
                        value = jnp.where(covers(begins_in[p], limit, t), part, value)
                        value = jnp.where(covers(limit, begins_in[p + 1], t), rests[p], value)
                dst[to : to + size, B * t : B * (t + 1)] = value
            return
        h = size // 2
        for m in range(NQ // 2):
            lo, hi = 2 * m, 2 * m + 1
            cols = [slice(B * (3 * m + t), B * (3 * m + t + 1)) for t in range(3)]
            dst[to : to + size, cols[0]] = read(lo, 0, size)
            dst[to : to + size, cols[2]] = read(hi, 0, size)
            a, b = read(lo, size, h), read(hi, size, h)
            dst[to : to + h, cols[1]] = jnp.where(line < B // 2, a, b)
            dst[to + h : to + size, cols[1]] = pltpu.roll(
                jnp.where(line < B // 2, b, a), B // 2, 1
            )

    def assemble_edge():
        if not even:
            assemble(edge, 0, HALO, lambda p, r, n: own[p, r : r + n, :])
            return
        for m in range(NQ // 2):
            lo, hi = own[2 * m, 0:HALO, :], own[2 * m + 1, 0:HALO, :]
            at = 3 * m * B
            edge[0:4, at : at + B] = lo[0:4]
            edge[0:4, at + B : at + 2 * B] = jnp.where(line < B // 2, lo, hi)[4:8]
            edge[0:4, at + 2 * B : at + 3 * B] = hi[0:4]

    for t in range(KX):
        scale[0:1, B * t : B * (t + 1)] = spacing[t : t + 1, :]
    at = lax.broadcasted_iota(jnp.int32, (16, NX), 1)
    per_out = 2 * 48 + (REST if wide_out else 0)
    group16 = lax.broadcasted_iota(jnp.int32, (REST, B), 1) // 32
    z_copies, m_copies = {}, {}
    for chunk, (first, size) in enumerate(CHUNKS):
        for s in ORDER:
            from_q = (q + NQ - s) % NQ
            if s:
                o_copies[chunk, s].wait_recv()
            else:
                o_copies[chunk, s].wait()
            cp = remote(
                own.at[from_q, lay.inner(chunk)], mate.at[from_q, lay.bare(chunk)],
                m_send.at[chunk, s], m_recv.at[chunk, s], row, twin,
            )
            cp.start()
            m_copies[chunk, s] = cp
        if chunk == 0:
            assemble_edge()
            field[HALO - 1 : HALO, :] = edge[0:1, :]
            field[HALO + ZL : HALO + ZL + 1, :] = edge[1:2, :]
        o_at, c_at = lay.halo + lay.at[chunk], lay.at[chunk]
        assemble(
            field, first + HALO, size, lambda p, r, n: own[p, o_at + r : o_at + r + n, :]
        )
        if chunk == 0:
            for cp in loads[1:]:
                cp.wait()
        for s in range(NQ):
            c_copies[chunk, s].wait_recv()
            m_copies[chunk, s].wait_recv()
        assemble(
            diff, first, size,
            lambda p, r, n: (
                mate[p, c_at + r : c_at + r + n, :] - cross[p, c_at + r : c_at + r + n, :]
            ) * sign,
        )
        first, size = STEPS[chunk]
        rows = slice(first, first + size)
        for r in range(first, first + size, 16):
            r0 = r + HALO
            here_f = field[r0 : r0 + 16, :]
            low = jnp.where(at == 0, 0.0, pltpu.roll(here_f, 1, 1))
            high = jnp.where(at == NX - 1, 0.0, pltpu.roll(here_f, NX - 1, 1))
            grad_z = field[r0 + 1 : r0 + 17, :] - field[r0 - 1 : r0 + 15, :]
            u, v, w = [vel[j, r : r + 16, :].astype(F32) for j in range(3)]
            advection = u * ((high - low) * scale[0:1, :])
            advection += 0.5 * (v * diff[r : r + 16, :]) + 0.5 * (w * grad_z)
            right[r : r + 16, :] = here_f - advection
        end = None
        for k in range(KX):
            across_k = inverse[k].T
            y = jnp.dot(
                right[rows, B * k : B * (k + 1)], across_k, precision=HIGH,
                preferred_element_type=F32,
            )
            if k:
                y = y + (link[k - 1] * across_k[0:1, :]) * end
            if k < KX - 1:
                coef[k : k + 1, :] = link[k] * across_k[B - 1 : B, :]
            end = y[:, B - 1 : B]
            solved[rows, B * k : B * (k + 1)] = y
        head = None
        for k in reversed(range(KX)):
            y = solved[rows, B * k : B * (k + 1)]
            if k < KX - 1:
                y = y + coef[k : k + 1, :] * head
                solved[rows, B * k : B * (k + 1)] = y
            head = y[:, 0:1]
        out_at = per_out * chunk
        for p in range(NQ):
            limit = jnp.minimum(begins_out[p] + RING, begins_out[p + 1])
            values = [jnp.zeros((size, B), F32) for _ in range(2)]
            rest = jnp.zeros((size, B), F32)
            for t in quad_tiles(p, most):
                tile = solved[rows, B * t : B * (t + 1)]
                values[t % 2] = jnp.where(covers(begins_out[p], limit, t), tile, values[t % 2])
                if wide_out:
                    rest = jnp.where(covers(limit, begins_out[p + 1], t), tile, rest)
            for b in range(2):
                packed[p, out_at + size * b : out_at + size * (b + 1), :] = values[b]
            if wide_out:
                rest = fold(rest)
                tight = rest[2 * REST : 3 * REST]
                for g in (1, 0):
                    tight = jnp.where(group16 == g, rest[REST * g : REST * (g + 1)], tight)
                packed[p, out_at + 2 * size : out_at + 2 * size + REST, :] = tight
        for s in ORDER[:-1]:
            to_q = (q + s) % NQ
            cp = remote(
                packed.at[to_q, pl.ds(out_at, per_out)], rz.at[q, pl.ds(out_at, per_out)],
                z_send.at[chunk, s], z_recv.at[chunk, s], QX * to_q + x, c,
            )
            cp.start()
            z_copies[chunk, s] = cp

    pieces, rests = [], []
    limit = start_at(counts_out, QX * q) + RING
    for i in range(QX):
        at_row = QX * q + (x + i) % QX
        begin, count = start_at(counts_out, at_row), counts_out[at_row]
        inner = jnp.minimum(jnp.maximum(limit - begin, 0), count)
        pieces.append(slot_masks(2, begin, inner, lane))
        rests.append(slot_masks(1, begin + inner, count - inner, lane)[0])
    y_copies = []
    for chunk, (first, size) in enumerate(STEPS):
        out_at = per_out * chunk
        for s in (0,) + ORDER[:-1]:
            from_q = (q + NQ - s) % NQ
            if s:
                z_copies[chunk, s].wait_recv()

            def step(j, carry):
                r = pl.multiple_of(8 * j, 8)

                def read(to):
                    if s:
                        return rz[from_q, pl.ds(out_at + to + r, 8), :]
                    return packed[q, pl.ds(out_at + to + r, 8), :]

                for g in range(size // REST):
                    parts = [read(REST * g), read(size + REST * g)]
                    if wide_out:
                        parts.append(fold(jnp.where(group == g, read(2 * size), 0.0)))
                    for d in range(QX):
                        masks = pieces[d] + ([rests[d]] if wide_out else [])
                        piece[d, s, pl.ds(first + REST * g + r, 8), :] = choose(masks, parts)
                return carry

            lax.fori_loop(0, REST // 8, step, 0)
            to = pl.multiple_of(ZL * (QX * from_q + x) + first, 8)
            for d in range(QX):
                part, goal = piece.at[d, s, pl.ds(first, size)], out.at[pl.ds(to, size), :]
                if d:
                    cp = remote(
                        part, goal, y_send.at[chunk, d, s], y_recv.at[chunk, d, s],
                        QX * q + (x + d) % QX, c,
                    )
                else:
                    cp = pltpu.make_async_copy(part, goal, y_local.at[chunk, s])
                cp.start()
                y_copies.append(cp)
    for cp in y_copies:
        cp.wait()
    for chunk in range(NC):
        for s in range(NQ):
            m_copies[chunk, s].wait_send()
            c_copies[chunk, s].wait_send()
            if s:
                o_copies[chunk, s].wait_send()
                z_copies[chunk, s].wait_send()
    for chunk, s in todo:
        for d, cp in x_copies[chunk, s]:
            if d:
                cp.wait_send()
        if even:
            pl.when(q < NQ - 1)(n_copies[0, chunk, s].wait_send)
            pl.when(q > 0)(n_copies[1, chunk, s].wait_send)


def flow(even, wide_out, cid, counts_in, counts_out, link, temp, vel, spacing, inverse):
    dma = pltpu.SemaphoreType.DMA
    vmem = pl.BlockSpec(memory_space=pltpu.VMEM)
    smem = pl.BlockSpec(memory_space=pltpu.SMEM)
    hbm = pl.BlockSpec(memory_space=pl.ANY)
    per = dma((NC, NQ))
    lay = EVEN if even else WIDE
    per_out = NC * (2 * 48 + (REST if wide_out else 0))
    return pl.pallas_call(
        functools.partial(flow_kernel, even, wide_out),
        name="flow%d%d" % (even, wide_out),
        out_shape=jax.ShapeDtypeStruct((KZ * B, B), F32),
        in_specs=[smem, smem, smem, hbm, hbm, vmem, hbm],
        out_specs=hbm,
        scratch_shapes=[
            pltpu.VMEM((SLOTS * KZ, B), F32),
            pltpu.VMEM((2, 2 * B, B), F32),
            pltpu.VMEM((KZ * B + 2 * HALO, B), F32),
            pltpu.VMEM((QX, NQ, SPAN, B), F32),
            pltpu.VMEM((NQ, lay.halo + lay.total, B), F32),
            pltpu.VMEM((NQ, lay.halo + lay.total, B), F32),
            pltpu.VMEM((NQ, lay.total, B), F32),
            pltpu.VMEM((NQ, lay.total, B), F32),
            pltpu.VMEM((2, NQ, SPAN, B), F32),
            pltpu.VMEM((2, NQ, SPAN, B), F32),
            pltpu.VMEM((3, ZL, NX), jnp.bfloat16),
            pltpu.VMEM((KX, B, B), F32),
            pltpu.VMEM((SPAN, NX), F32),
            pltpu.VMEM((HALO, NX), F32),
            pltpu.VMEM((ZL, NX), F32),
            pltpu.VMEM((ZL, NX), F32),
            pltpu.VMEM((ZL, NX), F32),
            pltpu.VMEM((KX + 4, B), F32),
            pltpu.VMEM((HALO, NX), F32),
            pltpu.VMEM((NQ, per_out, B), F32),
            pltpu.VMEM((NQ, per_out, B), F32),
            pltpu.VMEM((QX, NQ, ZL, B), F32),
            dma((3,)), dma((NC + 1, QX, NQ)), dma((NC + 1, QX, NQ)), dma((NC + 1, NQ)),
            per, per, dma((NC,)), per, per, per, per,
            dma((2, NC, NQ)), dma((2, NC, NQ)), per, per,
            dma((NC, QX, NQ)), dma((NC, QX, NQ)), per,
        ],
        compiler_params=pltpu.CompilerParams(
            collective_id=cid, has_side_effects=True, vmem_limit_bytes=LIMIT
        ),
    )(counts_in, counts_out, link, temp, vel, spacing, inverse)


def last_kernel(counts, link, lines_hbm, inverse, out, lines, solved, doubled, load):
    q, x, _ = here()
    row = QX * q + x
    off = start_at(counts, row) % B
    valid = lax.broadcasted_iota(jnp.int32, (SLOTS, B), 0) < counts[row]
    parts = []
    for n in range(PARTS):
        rows = pl.ds(KZ * B // PARTS * n, KZ * B // PARTS)
        parts.append(pltpu.make_async_copy(lines_hbm.at[rows], lines.at[rows], load.at[n]))
        parts[n].start()
    end = None
    for k in range(KZ):
        if k % (KZ // PARTS) == 0:
            parts[k // (KZ // PARTS)].wait()
        y = jnp.dot(
            inverse[k], lines[B * k : B * (k + 1), :], precision=HIGH,
            preferred_element_type=F32,
        )
        if k:
            y = y + (link[k - 1] * inverse[k, :, 0:1]) * end
        end = y[B - 1 : B, :]
        solved[B * k : B * (k + 1), :] = y
    head = None
    for k in reversed(range(KZ)):
        y = solved[B * k : B * (k + 1), :]
        if k < KZ - 1:
            y = y + (link[k] * inverse[k, :, B - 1 : B]) * head
        head = y[0:1, :]
        turned, j = y.T, k % 4
        doubled[j, 0:B, :] = turned
        doubled[j, B : B + SLOTS, :] = turned[0:SLOTS]
        mine = doubled[j, pl.ds(off, SLOTS), :]
        out[pl.ds(k, SLOTS, stride=KZ), :] = jnp.where(valid, mine, 0.0)


def on_device(
    temp_in, velocity, spacing_x, inverse_x, link_x, inverse_z, link_z, counts_in, counts_out
):
    vmem = pl.BlockSpec(memory_space=pltpu.VMEM)
    smem = pl.BlockSpec(memory_space=pltpu.SMEM)
    local = pltpu.CompilerParams(vmem_limit_bytes=LIMIT)
    pick = pl.pallas_call(
        pick_kernel,
        name="pick",
        out_shape=jax.ShapeDtypeStruct((1,), jnp.int32),
        in_specs=[smem, smem],
        out_specs=smem,
    )(counts_in, counts_out)
    lines = lax.switch(
        pick[0],
        [
            functools.partial(flow, even, wide_out, 1 + i)
            for i, (even, wide_out) in enumerate(((1, 0), (1, 1), (0, 1)))
        ],
        counts_in, counts_out, link_x, temp_in.reshape(SLOTS * KZ, B),
        velocity.reshape(3, ZL, NX), spacing_x.reshape(KX, B), inverse_x,
    )
    out = pl.pallas_call(
        last_kernel,
        name="last",
        out_shape=jax.ShapeDtypeStruct((SLOTS * KZ, B), F32),
        in_specs=[smem, smem, pl.BlockSpec(memory_space=pl.ANY), vmem],
        out_specs=vmem,
        scratch_shapes=[
            pltpu.VMEM((KZ * B, B), F32),
            pltpu.VMEM((KZ * B, B), F32),
            pltpu.VMEM((4, 2 * B, B), F32),
            pltpu.SemaphoreType.DMA((PARTS,)),
        ],
        compiler_params=local,
    )(counts_out, link_z, lines, inverse_z)
    return out.reshape(SLOTS, 1, KZ * B)


def solution(mesh):
    in_specs = (
        P("row", "col", None),
        P(None, "col", "row", None),
        P(),
        P(),
        P(),
        P(),
        P(),
        P(),
        P(),
    )
    out_specs = P("row", "col", None)
    return jax.shard_map(
        on_device, mesh=mesh, in_specs=in_specs, out_specs=out_specs, check_vma=False
    )
```
